128 devices in a mesh: outer: 4 (over x_hi, core), inner: 32 (over y, z, x_lo).
Axes of the slice: x: 4 (x_hi: 2, x_lo: 2; x = x_hi * 2 + x_lo), y: 4, z: 4, core: 2. Of those that a mesh axis runs over, the one named last changes fastest.
Arguments:
- queries: bfloat16 [32768, 1024], P(('outer', 'inner'))
- keys: bfloat16 [32768, 128], P(('outer', 'inner'))
- values: bfloat16 [32768, 128], P(('outer', 'inner')), may hold values from -6 to 6
- positions: int32 [32768], P(('outer', 'inner')), may hold values from 0 to 32767, as said below
Outputs:
- attended: bfloat16 [32768, 1024], P(('outer', 'inner'))
The draws below stay inside these ranges and needn't reach their ends.
Inputs may be any that keep to these rules, and one draw needn't show every extreme that they name: The stored tokens form 32768 // 256 consecutive groups of 256 rows, one group a device; each group's first 128 rows hold the positions b * (128) onward in increasing order by one, and its last 128 rows the positions from (255 - b) * (128) onward likewise, for a b below 128 that each group has for itself; every position occurs once.
All inputs are finite; a program needn't handle non-finite values.
Results may differ from the reference program's by a relative error of at most 0.0055.
Values may be sent and summed in bfloat16 or wider, within the bound.
No kernel may reach another device: no remote copies, remote signals or barrier semaphores. Data moves between devices by JAX's collectives and lax.ppermute only.
A program may use at most 128 MiB of HBM per device.

```python
import math
import jax
import jax.numpy as jnp
from jax import lax

H = 8
HD = 128
TOK_DEV = 256
TOKENS = 32768


def shared_keys(key):
    base = jax.random.normal(key, (TOKENS, HD), jnp.float32)
    half = TOK_DEV // 2
    rowidx = jnp.arange(TOKENS)
    chosen = rowidx % half == half - 2
    following = jnp.roll(base, -1, axis=0)
    return jnp.where(chosen[:, None], 0.99 * following, base)


def draw_keys(key, part):
    return shared_keys(key).astype(jnp.bfloat16)


def draw_queries(key, part):
    key = jax.random.fold_in(key, 3)
    return (3.0 * jax.random.normal(key, (TOKENS, H * HD), jnp.float32)).astype(jnp.bfloat16)


def draw_positions(key, part):
    key = jax.random.fold_in(key, 7)
    groups = TOKENS // TOK_DEV
    half = TOK_DEV // 2
    order = jax.random.permutation(key, groups).astype(jnp.int32)
    offsets = jnp.arange(half, dtype=jnp.int32)
    lower = order[:, None] * half + offsets[None, :]
    upper = (2 * groups - 1 - order)[:, None] * half + offsets[None, :]
    return jnp.stack([lower, upper], axis=1).reshape(TOKENS).astype(jnp.int32)


def level_of(rng, dims, shards, least, top_value):
    factor_of = 1.0
    for axis_at, shards_of in shards:
        steps = jax.random.uniform(jax.random.fold_in(jax.random.fold_in(rng, 6), axis_at), (shards_of,), jnp.float32, least / len(shards), top_value / len(shards))
        factor_of = factor_of * jnp.repeat(jnp.exp(steps), dims[axis_at] // shards_of).reshape((-1,) + (1,) * (len(dims) - 1 - axis_at))
    return factor_of


def gaussian(stream_key, extent, spread, reach, cuts=(), held_as=jnp.bfloat16):
    array = jax.random.normal(stream_key, extent, jnp.float32) * spread
    if len(cuts) > 0:
        array = level_of(stream_key, extent, cuts, -0.22, 0.18) * array
    return jnp.clip(array, min=-reach, max=reach).astype(held_as)


def setup_inputs(seed: int = 0) -> dict:
    splits = jax.random.split(jax.random.key(seed), 5)
    return {
        "queries": draw_queries(jax.random.fold_in(splits[4], 71), 0),
        "keys": draw_keys(jax.random.fold_in(splits[4], 71), 0),
        "values": gaussian(splits[2], (TOKENS, HD), 1.0, 6.0, ((0, 128),)),
        "positions": draw_positions(jax.random.fold_in(splits[4], 71), 0),
    }


def reference(queries, keys, values, positions):
    block = math.gcd(TOKENS, 128)
    scale = HD ** -0.5
    query_blocks = queries.reshape(TOKENS // block, block, H * HD)
    pos_blocks = positions.reshape(TOKENS // block, block)

    def one_block(pair):
        query_rows, query_pos = pair
        rows = query_rows.reshape(block * H, HD)
        row_pos = jnp.repeat(query_pos, H)
        scores = lax.dot_general(rows, keys, (((1,), (1,)), ((), ())), preferred_element_type=jnp.float32) * scale
        visible = positions[None, :] <= row_pos[:, None]
        scores = jnp.where(visible, scores, jnp.float32(-1.0e30))
        best = jnp.max(scores, axis=1)
        expd = jnp.where(visible, jnp.exp(scores - best[:, None]), jnp.float32(0.0))
        total = jnp.sum(expd, axis=1)
        numer = jnp.dot(expd.astype(jnp.bfloat16), values, preferred_element_type=jnp.float32)
        result = (numer / total[:, None]).astype(jnp.bfloat16)
        return result.reshape(block, H * HD)

    out = lax.map(one_block, (query_blocks, pos_blocks))
    return out.reshape(TOKENS, H * HD)
```

```python
import functools
import math

import jax
import jax.numpy as jnp
from jax import lax
from jax.experimental import pallas as pl
from jax.experimental.pallas import tpu as pltpu
from jax.sharding import PartitionSpec as P

AXES = ("outer", "inner")
RUN = 128
HD = 128
HEADS = 8
ROWS = RUN * HEADS
SHARD = 4 * RUN + 16
QROWS = 2 * RUN + 16
ACC = HD + 16
GROUP = 8
COEF = HD**-0.5 * math.log2(math.e)
NEG = -1e30
LIMIT = 2.0**100
VMEM_BYTES = 56 * 2**20


def dot(a, b, ca, cb):
    return lax.dot_general(a, b, (((ca,), (cb,)), ((), ())), preferred_element_type=jnp.float32)


def split3(x):
    hi = x.astype(jnp.bfloat16)
    rest = x - hi.astype(jnp.float32)
    mid = rest.astype(jnp.bfloat16)
    low = (rest - mid.astype(jnp.float32)).astype(jnp.bfloat16)
    return hi, mid, low


def stack_rows(rows, width):
    at = lax.broadcasted_iota(jnp.int32, (16, width), 0)
    tile = jnp.zeros((16, width), jnp.float32)
    for i, row in enumerate(rows):
        tile = jnp.where(at == i, row.astype(jnp.float32), tile)
    return tile.astype(jnp.bfloat16)


def pack_kv_kernel(pos_ref, key_ref, value_ref, out_ref):
    out_ref[0 : 2 * RUN, :] = key_ref[...]
    for half in range(2):
        v = value_ref[half * RUN : (half + 1) * RUN, :].astype(jnp.float32)
        out_ref[(2 + half) * RUN : (3 + half) * RUN, :] = v.T.astype(jnp.bfloat16)
    block = (pos_ref[0] // RUN).astype(jnp.float32)
    out_ref[4 * RUN : SHARD, :] = jnp.full((16, HD), block, jnp.float32).astype(jnp.bfloat16)


def pack_kv(positions, keys, values):
    return pl.pallas_call(
        pack_kv_kernel,
        out_shape=jax.ShapeDtypeStruct((SHARD, HD), jnp.bfloat16),
        in_specs=[
            pl.BlockSpec(memory_space=pltpu.SMEM),
            pl.BlockSpec(memory_space=pltpu.VMEM),
            pl.BlockSpec(memory_space=pltpu.VMEM),
        ],
        out_specs=pl.BlockSpec(memory_space=pltpu.VMEM),
        name="pack_kv",
    )(positions, keys, values)


def query_tile(ref, half):
    rows = slice(half * RUN, (half + 1) * RUN)
    return jnp.concatenate([ref[rows, h * HD : (h + 1) * HD] for h in range(HEADS)], axis=0)


def pack_q_kernel(query_ref, shard_ref, out_ref, acc_ref):
    out_ref[0 : 2 * RUN, :] = query_ref[...]
    shifts = []
    key_at = lax.broadcasted_iota(jnp.int32, (RUN, ROWS), 0)
    row_at = lax.broadcasted_iota(jnp.int32, (RUN, ROWS), 1) % RUN
    ones = jnp.ones((16, RUN), jnp.bfloat16)
    for half in range(2):
        scores = dot(shard_ref[half * RUN : (half + 1) * RUN, :], query_tile(query_ref, half), 1, 1)
        scores = jnp.where(key_at <= row_at, scores * COEF, NEG)
        shift = jnp.max(scores, axis=0, keepdims=True)
        weights = jnp.exp2(scores - shift).astype(jnp.bfloat16)
        vt = jnp.concatenate([shard_ref[(2 + half) * RUN : (3 + half) * RUN, :], ones], axis=0)
        acc_ref[:, half * ROWS : (half + 1) * ROWS] = dot(vt, weights, 1, 0)
        shifts.append(shift)
    block = jnp.concatenate([shard_ref[4 * RUN : 4 * RUN + 1, :]] * HEADS, axis=1)
    out_ref[2 * RUN : QROWS, :] = stack_rows(split3(shifts[0]) + split3(shifts[1]) + (block,), ROWS)


def pack_q(queries, shard):
    return pl.pallas_call(
        pack_q_kernel,
        out_shape=(
            jax.ShapeDtypeStruct((QROWS, ROWS), jnp.bfloat16),
            jax.ShapeDtypeStruct((ACC, 2 * ROWS), jnp.float32),
        ),
        in_specs=[pl.BlockSpec(memory_space=pltpu.VMEM)] * 2,
        out_specs=(pl.BlockSpec(memory_space=pltpu.VMEM),) * 2,
        compiler_params=pltpu.CompilerParams(vmem_limit_bytes=VMEM_BYTES),
        name="pack_q",
    )(queries, shard)


def attend_kernel(count, shards, own, *refs):
    q_refs = refs[:count]
    kv_ref = refs[count]
    at = count + 1
    acc0_ref = None
    if own:
        acc0_ref = refs[at]
        at += 1
    out_refs = refs[at : at + count]
    q_buf, m_buf, acc_ref, ints, blocks, tasks, sem = refs[at + count :]
    total = 2 * shards

    for i in range(shards):
        row = kv_ref[i * SHARD + 4 * RUN : i * SHARD + SHARD, :].astype(jnp.float32)[0:1]
        ints[i : i + 1, :] = row.astype(jnp.int32)
    for j in range(count):
        row = q_refs[j][2 * RUN : QROWS, 0:HD].astype(jnp.float32)[6:7]
        ints[shards + j : shards + j + 1, :] = row.astype(jnp.int32)
    copy = pltpu.make_async_copy(ints, blocks, sem)
    copy.start()
    copy.wait()

    def key_block(task):
        shard = task // 2
        start = pl.multiple_of(shard * SHARD + (task - 2 * shard) * RUN, 16)
        return kv_ref[pl.ds(start, RUN), :]

    def value_block(task):
        shard = task // 2
        start = pl.multiple_of(shard * SHARD + (2 + task - 2 * shard) * RUN, 16)
        return kv_ref[pl.ds(start, RUN), :]

    ones = jnp.ones((16, GROUP * RUN), jnp.bfloat16)

    for j in range(count):
        q_ref = q_refs[j]
        here = blocks[shards + j, 0]
        tail = q_ref[2 * RUN : QROWS, :].astype(jnp.float32)
        for half in range(2):
            q_buf[half] = query_tile(q_ref, half)
            m_buf[half] = jnp.broadcast_to(
                tail[3 * half : 3 * half + 1]
                + tail[3 * half + 1 : 3 * half + 2]
                + tail[3 * half + 2 : 3 * half + 3],
                (8, ROWS),
            )
            if own:
                acc_ref[half] = acc0_ref[:, half * ROWS : (half + 1) * ROWS]
            else:
                acc_ref[half] = jnp.zeros((ACC, ROWS), jnp.float32)

        def place(i, ends):
            low, high = ends
            block = blocks[i, 0]
            tasks[high] = 2 * i
            high = high - 1
            later = block > here
            tasks[jnp.where(later, high, total)] = 2 * i + 1
            high = high - later.astype(jnp.int32)
            earlier = block < here
            tasks[jnp.where(earlier, low, total)] = 2 * i
            low = low + earlier.astype(jnp.int32)
            return low, high

        for i in range(total):
            tasks[i] = 0
        low_end, high_end = lax.fori_loop(0, shards, place, (jnp.int32(0), jnp.int32(total - 1)))
        high_start = high_end + 1

        def pure(first, half):
            query = q_buf[half]
            shift = m_buf[half][0:1]
            parts = []
            for b in range(0, GROUP, 2):
                keys = jnp.concatenate([key_block(tasks[first + b]), key_block(tasks[first + b + 1])], axis=0)
                parts.append(jnp.exp2(dot(keys, query, 1, 1) * COEF - shift).astype(jnp.bfloat16))
            weights = jnp.concatenate(parts, axis=0)
            vt = jnp.concatenate([value_block(tasks[first + b]) for b in range(GROUP)], axis=1)
            vt = jnp.concatenate([vt, ones], axis=0)
            acc_ref[half] += dot(vt, weights, 1, 0)

        def mixed(first):
            parts = []
            for b in range(GROUP):
                half = (first + b >= high_start).astype(jnp.int32)
                scores = dot(key_block(tasks[first + b]), q_buf[half], 1, 1)
                parts.append(jnp.exp2(scores * COEF - m_buf[half][0:1]).astype(jnp.bfloat16))
            weights = jnp.concatenate(parts, axis=0)
            vt = jnp.concatenate([value_block(tasks[first + b]) for b in range(GROUP)], axis=1)
            vt = jnp.concatenate([vt, ones], axis=0)
            index = first + lax.broadcasted_iota(jnp.int32, (1, GROUP * RUN), 1) // RUN
            zero = jnp.zeros((), jnp.bfloat16)
            acc_ref[0] += dot(jnp.where(index < low_end, vt, zero), weights, 1, 0)
            acc_ref[1] += dot(jnp.where(index >= high_start, vt, zero), weights, 1, 0)

        @pl.loop(0, total // GROUP)
        def _(g):
            first = g * GROUP
            is_low = first + GROUP <= low_end
            is_high = first >= high_start

            @pl.when(jnp.logical_or(is_low, is_high))
            def _():
                pure(first, is_high.astype(jnp.int32))

            @pl.when(jnp.logical_not(jnp.logical_or(is_low, is_high)))
            def _():
                mixed(first)

        sums = jnp.maximum(acc_ref[0][HD : HD + 8], acc_ref[1][HD : HD + 8])
        fine = jnp.min(jnp.where(sums < LIMIT, 1.0, 0.0)) > 0.5

        @pl.when(jnp.logical_not(fine))
        def _():
            for half in range(2):
                if own:
                    acc_ref[half] = acc0_ref[:, half * ROWS : (half + 1) * ROWS]
                else:
                    acc_ref[half] = jnp.zeros((ACC, ROWS), jnp.float32)

            @pl.loop(0, total)
            def _(t):
                @pl.when(jnp.logical_or(t < low_end, t >= high_start))
                def _():
                    half = (t >= high_start).astype(jnp.int32)
                    scores = dot(key_block(tasks[t]), q_buf[half], 1, 1) * COEF
                    old = m_buf[half][0:1]
                    new = jnp.maximum(old, jnp.max(scores, axis=0, keepdims=True))
                    weights = jnp.exp2(scores - new).astype(jnp.bfloat16)
                    vt = jnp.concatenate([value_block(tasks[t]), ones[:, :RUN]], axis=0)
                    acc_ref[half] = acc_ref[half] * jnp.exp2(old - new) + dot(vt, weights, 1, 0)
                    m_buf[half] = jnp.broadcast_to(new, (8, ROWS))

        for half in range(2):
            span = slice(half * ROWS, (half + 1) * ROWS)
            if own:
                out_refs[j][0 : HD + 8, span] = acc_ref[half][0 : HD + 8]
                out_refs[j][HD + 8 : ACC, span] = m_buf[half]
            else:
                acc = acc_ref[half]
                out_refs[j][0:HD, span] = acc[0:HD].astype(jnp.bfloat16)
                out_refs[j][HD:ACC, span] = stack_rows(
                    split3(acc[HD : HD + 1]) + split3(m_buf[half][0:1]), ROWS
                )


def attend(q_list, kv, acc0=None):
    count, shards = len(q_list), kv.shape[0] // SHARD
    own = acc0 is not None
    int_rows = -(-(shards + count) // 8) * 8
    args = tuple(q_list) + (kv,) + ((acc0,) if own else ())
    out = jax.ShapeDtypeStruct((ACC, 2 * ROWS), jnp.float32 if own else jnp.bfloat16)
    pairs = count * 2 * shards * RUN * ROWS
    return pl.pallas_call(
        functools.partial(attend_kernel, count, shards, own),
        out_shape=(out,) * count,
        in_specs=[pl.BlockSpec(memory_space=pltpu.VMEM)] * len(args),
        out_specs=(pl.BlockSpec(memory_space=pltpu.VMEM),) * count,
        scratch_shapes=[
            pltpu.VMEM((2, ROWS, HD), jnp.bfloat16),
            pltpu.VMEM((2, 8, ROWS), jnp.float32),
            pltpu.VMEM((2, ACC, ROWS), jnp.float32),
            pltpu.VMEM((int_rows, HD), jnp.int32),
            pltpu.SMEM((int_rows, HD), jnp.int32),
            pltpu.SMEM((2 * shards + 8,), jnp.int32),
            pltpu.SemaphoreType.DMA,
        ],
        compiler_params=pltpu.CompilerParams(vmem_limit_bytes=VMEM_BYTES),
        cost_estimate=pl.CostEstimate(flops=pairs * HD * 8, bytes_accessed=8 << 20, transcendentals=pairs),
        name="attend",
    )(*args)


def combine_kernel(own_ref, one_ref, two_ref, three_ref, out_ref):
    for half in range(2):
        for h in range(HEADS):
            span = slice(half * ROWS + h * RUN, half * ROWS + (h + 1) * RUN)
            parts = [(own_ref[0:HD, span], own_ref[HD : HD + 1, span], own_ref[HD + 8 : HD + 9, span])]
            for ref in (one_ref, two_ref, three_ref):
                tail = ref[HD:ACC, span].astype(jnp.float32)
                parts.append(
                    (
                        ref[0:HD, span].astype(jnp.float32),
                        tail[0:1] + tail[1:2] + tail[2:3],
                        tail[3:4] + tail[4:5] + tail[5:6],
                    )
                )
            top = functools.reduce(jnp.maximum, [p[2] for p in parts])
            factors = [jnp.exp2(p[2] - top) for p in parts]
            numer = sum(p[0] * f for p, f in zip(parts, factors))
            total = sum(p[1] * f for p, f in zip(parts, factors))
            out_ref[half * RUN : (half + 1) * RUN, h * HD : (h + 1) * HD] = (
                (numer / total).T.astype(jnp.bfloat16)
            )


def combine(own, others):
    return pl.pallas_call(
        combine_kernel,
        out_shape=jax.ShapeDtypeStruct((2 * RUN, ROWS), jnp.bfloat16),
        in_specs=[pl.BlockSpec(memory_space=pltpu.VMEM)] * 4,
        out_specs=pl.BlockSpec(memory_space=pltpu.VMEM),
        compiler_params=pltpu.CompilerParams(vmem_limit_bytes=VMEM_BYTES),
        name="combine",
    )(own, *others)


def place_of(x, y, z, core):
    return ((x // 2) * 2 + core) * 32 + (y * 4 + z) * 2 + x % 2


def swap(array, flips):
    pairs = []
    for x in range(4):
        for y in range(4):
            for z in range(4):
                for core in range(2):
                    dx, dy, dz, dc = flips(core)
                    pairs.append((place_of(x, y, z, core), place_of(x ^ dx, y ^ dy, z ^ dz, core ^ dc)))
    return lax.ppermute(array, AXES, pairs)


def ring_x(array, step):
    return swap(array, lambda core: (step, 0, 0, 0))


def ring_first(array, step):
    return swap(array, lambda core: (0, step, 0, 0) if core else (0, 0, step, 0))


def ring_second(array, step):
    return swap(array, lambda core: (0, 0, step, 0) if core else (0, step, 0, 0))


def cores(array):
    return swap(array, lambda core: (0, 0, 0, 1))


STEPS = (1, 3, 2)


def body(queries, keys, values, positions):
    shard = pack_kv(positions, keys, values)
    near = [ring_first(shard, s) for s in STEPS]
    packed, acc0 = pack_q(queries, shard)
    others = [ring_x(packed, s) for s in STEPS]
    line = jnp.concatenate([shard] + near, axis=0)
    far = [ring_second(line, s) for s in STEPS]
    plane = jnp.concatenate([line] + far, axis=0)
    kv = jnp.concatenate([plane, cores(plane)], axis=0)
    part1, part3 = attend(others[:2], kv)
    back1, back3 = ring_x(part1, 1), ring_x(part3, 3)
    (part2,) = attend(others[2:], kv)
    back2 = ring_x(part2, 2)
    (mine,) = attend([packed], kv, acc0)
    return combine(mine, (back1, back3, back2))


def solution(mesh):
    return jax.shard_map(
        body,
        mesh=mesh,
        in_specs=(P(AXES, None), P(AXES, None), P(AXES, None), P(AXES)),
        out_specs=P(AXES, None),
        check_vma=False,
    )
```

```python
import functools
import math

import jax
import jax.numpy as jnp
from jax import lax
from jax.experimental import pallas as pl
from jax.experimental.pallas import tpu as pltpu
from jax.sharding import PartitionSpec as P

AXES = ("outer", "inner")
RUN = 128
HD = 128
HEADS = 8
ROWS = RUN * HEADS
SHARD = 4 * RUN + 16
QROWS = 2 * RUN + 16
ACC = HD + 16
GROUP = 8
COEF = HD**-0.5 * math.log2(math.e)
NEG = -1e30
LIMIT = 2.0**100
VMEM_BYTES = 56 * 2**20


def dot(a, b, ca, cb):
    return lax.dot_general(a, b, (((ca,), (cb,)), ((), ())), preferred_element_type=jnp.float32)


def split3(x):
    hi = x.astype(jnp.bfloat16)
    rest = x - hi.astype(jnp.float32)
    mid = rest.astype(jnp.bfloat16)
    low = (rest - mid.astype(jnp.float32)).astype(jnp.bfloat16)
    return hi, mid, low


def stack_rows(rows, width):
    at = lax.broadcasted_iota(jnp.int32, (16, width), 0)
    tile = jnp.zeros((16, width), jnp.float32)
    for i, row in enumerate(rows):
        tile = jnp.where(at == i, row.astype(jnp.float32), tile)
    return tile.astype(jnp.bfloat16)


def pack_kv_kernel(pos_ref, key_ref, value_ref, out_ref):
    out_ref[0 : 2 * RUN, :] = key_ref[...]
    for half in range(2):
        v = value_ref[half * RUN : (half + 1) * RUN, :].astype(jnp.float32)
        out_ref[(2 + half) * RUN : (3 + half) * RUN, :] = v.T.astype(jnp.bfloat16)
    block = (pos_ref[0] // RUN).astype(jnp.float32)
    out_ref[4 * RUN : SHARD, :] = jnp.full((16, HD), block, jnp.float32).astype(jnp.bfloat16)


def pack_kv(positions, keys, values):
    return pl.pallas_call(
        pack_kv_kernel,
        out_shape=jax.ShapeDtypeStruct((SHARD, HD), jnp.bfloat16),
        in_specs=[
            pl.BlockSpec(memory_space=pltpu.SMEM),
            pl.BlockSpec(memory_space=pltpu.VMEM),
            pl.BlockSpec(memory_space=pltpu.VMEM),
        ],
        out_specs=pl.BlockSpec(memory_space=pltpu.VMEM),
        name="pack_kv",
    )(positions, keys, values)


def query_tile(ref, half):
    rows = slice(half * RUN, (half + 1) * RUN)
    return jnp.concatenate([ref[rows, h * HD : (h + 1) * HD] for h in range(HEADS)], axis=0)


def pack_q_kernel(query_ref, shard_ref, out_ref, acc_ref):
    out_ref[0 : 2 * RUN, :] = query_ref[...]
    shifts = []
    key_at = lax.broadcasted_iota(jnp.int32, (RUN, ROWS), 0)
    row_at = lax.broadcasted_iota(jnp.int32, (RUN, ROWS), 1) % RUN
    ones = jnp.ones((16, RUN), jnp.bfloat16)
    for half in range(2):
        scores = dot(shard_ref[half * RUN : (half + 1) * RUN, :], query_tile(query_ref, half), 1, 1)
        scores = jnp.where(key_at <= row_at, scores * COEF, NEG)
        shift = jnp.max(scores, axis=0, keepdims=True)
        weights = jnp.exp2(scores - shift).astype(jnp.bfloat16)
        vt = jnp.concatenate([shard_ref[(2 + half) * RUN : (3 + half) * RUN, :], ones], axis=0)
        acc_ref[:, half * ROWS : (half + 1) * ROWS] = dot(vt, weights, 1, 0)
        shifts.append(shift)
    block = jnp.concatenate([shard_ref[4 * RUN : 4 * RUN + 1, :]] * HEADS, axis=1)
    out_ref[2 * RUN : QROWS, :] = stack_rows(split3(shifts[0]) + split3(shifts[1]) + (block,), ROWS)


def pack_q(queries, shard):
    return pl.pallas_call(
        pack_q_kernel,
        out_shape=(
            jax.ShapeDtypeStruct((QROWS, ROWS), jnp.bfloat16),
            jax.ShapeDtypeStruct((ACC, 2 * ROWS), jnp.float32),
        ),
        in_specs=[pl.BlockSpec(memory_space=pltpu.VMEM)] * 2,
        out_specs=(pl.BlockSpec(memory_space=pltpu.VMEM),) * 2,
        compiler_params=pltpu.CompilerParams(vmem_limit_bytes=VMEM_BYTES),
        name="pack_q",
    )(queries, shard)


def attend_kernel(count, sizes, old, have, base, final, *refs):
    q_refs = refs[:count]
    at = count
    piece_refs = refs[at : at + len(sizes)]
    at += len(sizes)
    in_refs = refs[at : at + count] if have else None
    at += count if have else 0
    base_ref = refs[at] if base else None
    at += 1 if base else 0
    out_refs = refs[at : at + count]
    kv_ref, q_buf, m_buf, acc_ref, ints, blocks, tasks, sems, sem = refs[at + count :]
    starts = [sum(sizes[:i]) for i in range(len(sizes) + 1)]
    shards = starts[-1]

    def piece_copy(i):
        there = kv_ref.at[pl.ds(starts[i] * SHARD, sizes[i] * SHARD), :]
        return pltpu.make_async_copy(piece_refs[i], there, sems.at[i])

    def read_blocks(first, last):
        for i in range(first, last):
            row = kv_ref[i * SHARD + 4 * RUN : i * SHARD + SHARD, :].astype(jnp.float32)[0:1]
            ints[i : i + 1, :] = row.astype(jnp.int32)
        copy = pltpu.make_async_copy(ints, blocks, sem)
        copy.start()
        copy.wait()

    for i in range(old, len(sizes)):
        piece_copy(i).start()
    for j in range(count):
        row = q_refs[j][2 * RUN : QROWS, 0:HD].astype(jnp.float32)[6:7]
        ints[shards + j : shards + j + 1, :] = row.astype(jnp.int32)

    def key_block(task):
        shard = task // 2
        start = pl.multiple_of(shard * SHARD + (task - 2 * shard) * RUN, 16)
        return kv_ref[pl.ds(start, RUN), :]

    def value_block(task):
        shard = task // 2
        start = pl.multiple_of(shard * SHARD + (2 + task - 2 * shard) * RUN, 16)
        return kv_ref[pl.ds(start, RUN), :]

    def list_tasks(here, first, last):
        total = 2 * (last - first)

        def place(i, ends):
            low, high = ends
            block = blocks[i, 0]
            tasks[high] = 2 * i
            high = high - 1
            later = block > here
            tasks[jnp.where(later, high, total)] = 2 * i + 1
            high = high - later.astype(jnp.int32)
            earlier = block < here
            tasks[jnp.where(earlier, low, total)] = 2 * i
            low = low + earlier.astype(jnp.int32)
            return low, high

        for i in range(total):
            tasks[i] = 2 * first
        low_end, high_end = lax.fori_loop(first, last, place, (jnp.int32(0), jnp.int32(total - 1)))
        return low_end, high_end + 1

    ones = jnp.ones((16, GROUP * RUN), jnp.bfloat16)

    for j in range(count):
        q_ref = q_refs[j]
        tail = q_ref[2 * RUN : QROWS, :].astype(jnp.float32)
        for half in range(2):
            span = slice(half * ROWS, (half + 1) * ROWS)
            q_buf[half] = query_tile(q_ref, half)
            m_buf[half] = jnp.broadcast_to(
                tail[3 * half : 3 * half + 1]
                + tail[3 * half + 1 : 3 * half + 2]
                + tail[3 * half + 2 : 3 * half + 3],
                (8, ROWS),
            )
            if have:
                acc_ref[half] = in_refs[j][:, span]
            elif base:
                acc_ref[half] = base_ref[:, span]
            else:
                acc_ref[half] = jnp.zeros((ACC, ROWS), jnp.float32)
        if j == 0:
            for i in range(old, len(sizes)):
                piece_copy(i).wait()
            read_blocks(starts[old], shards)
        here = blocks[shards + j, 0]
        low_end, high_start = list_tasks(here, starts[old], shards)

        def pure(first, half):
            query = q_buf[half]
            shift = m_buf[half][0:1]
            parts = []
            for b in range(0, GROUP, 2):
                keys = jnp.concatenate([key_block(tasks[first + b]), key_block(tasks[first + b + 1])], axis=0)
                parts.append(jnp.exp2(dot(keys, query, 1, 1) * COEF - shift).astype(jnp.bfloat16))
            weights = jnp.concatenate(parts, axis=0)
            vt = jnp.concatenate([value_block(tasks[first + b]) for b in range(GROUP)], axis=1)
            vt = jnp.concatenate([vt, ones], axis=0)
            acc_ref[half] += dot(vt, weights, 1, 0)

        def mixed(first):
            parts = []
            for b in range(GROUP):
                half = (first + b >= high_start).astype(jnp.int32)
                scores = dot(key_block(tasks[first + b]), q_buf[half], 1, 1)
                parts.append(jnp.exp2(scores * COEF - m_buf[half][0:1]).astype(jnp.bfloat16))
            weights = jnp.concatenate(parts, axis=0)
            vt = jnp.concatenate([value_block(tasks[first + b]) for b in range(GROUP)], axis=1)
            vt = jnp.concatenate([vt, ones], axis=0)
            index = first + lax.broadcasted_iota(jnp.int32, (1, GROUP * RUN), 1) // RUN
            zero = jnp.zeros((), jnp.bfloat16)
            acc_ref[0] += dot(jnp.where(index < low_end, vt, zero), weights, 1, 0)
            acc_ref[1] += dot(jnp.where(index >= high_start, vt, zero), weights, 1, 0)

        @pl.loop(0, 2 * (shards - starts[old]) // GROUP)
        def _(g):
            first = g * GROUP
            is_low = first + GROUP <= low_end
            is_high = first >= high_start

            @pl.when(jnp.logical_or(is_low, is_high))
            def _():
                pure(first, is_high.astype(jnp.int32))

            @pl.when(jnp.logical_not(jnp.logical_or(is_low, is_high)))
            def _():
                mixed(first)

        if not final:
            for half in range(2):
                out_refs[j][:, half * ROWS : (half + 1) * ROWS] = acc_ref[half]
            continue

        sums = jnp.maximum(acc_ref[0][HD : HD + 8], acc_ref[1][HD : HD + 8])
        fine = jnp.min(jnp.where(sums < LIMIT, 1.0, 0.0)) > 0.5

        @pl.when(jnp.logical_not(fine))
        def _():
            for i in range(old):
                piece_copy(i).start()
            for i in range(old):
                piece_copy(i).wait()
            read_blocks(0, starts[old])
            low_all, high_all = list_tasks(here, 0, shards)
            for half in range(2):
                if base:
                    acc_ref[half] = base_ref[:, half * ROWS : (half + 1) * ROWS]
                else:
                    acc_ref[half] = jnp.zeros((ACC, ROWS), jnp.float32)

            @pl.loop(0, 2 * shards)
            def _(t):
                @pl.when(jnp.logical_or(t < low_all, t >= high_all))
                def _():
                    half = (t >= high_all).astype(jnp.int32)
                    scores = dot(key_block(tasks[t]), q_buf[half], 1, 1) * COEF
                    before = m_buf[half][0:1]
                    new = jnp.maximum(before, jnp.max(scores, axis=0, keepdims=True))
                    weights = jnp.exp2(scores - new).astype(jnp.bfloat16)
                    vt = jnp.concatenate([value_block(tasks[t]), ones[:, :RUN]], axis=0)
                    acc_ref[half] = acc_ref[half] * jnp.exp2(before - new) + dot(vt, weights, 1, 0)
                    m_buf[half] = jnp.broadcast_to(new, (8, ROWS))

        for half in range(2):
            span = slice(half * ROWS, (half + 1) * ROWS)
            if base:
                out_refs[j][0 : HD + 8, span] = acc_ref[half][0 : HD + 8]
                out_refs[j][HD + 8 : ACC, span] = m_buf[half]
            else:
                acc = acc_ref[half]
                out_refs[j][0:HD, span] = acc[0:HD].astype(jnp.bfloat16)
                out_refs[j][HD:ACC, span] = stack_rows(
                    split3(acc[HD : HD + 1]) + split3(m_buf[half][0:1]), ROWS
                )


def attend(q_list, new, old=(), acc=None, base=None, final=True):
    count = len(q_list)
    pieces = (tuple(old) if final else ()) + tuple(new)
    skip = len(old) if final else 0
    sizes = tuple(p.shape[0] // SHARD for p in pieces)
    shards = sum(sizes)
    int_rows = -(-(shards + count) // 8) * 8
    vmem = pl.BlockSpec(memory_space=pltpu.VMEM)
    args = tuple(q_list) + pieces + (tuple(acc) if acc is not None else ()) + ((base,) if base is not None else ())
    extra = len(args) - count - len(pieces)
    out = jax.ShapeDtypeStruct((ACC, 2 * ROWS), jnp.bfloat16 if final and base is None else jnp.float32)
    pairs = count * 2 * sum(sizes[skip:]) * RUN * ROWS
    return pl.pallas_call(
        functools.partial(attend_kernel, count, sizes, skip, acc is not None, base is not None, final),
        out_shape=(out,) * count,
        in_specs=[vmem] * count + [pl.BlockSpec(memory_space=pl.ANY)] * len(pieces) + [vmem] * extra,
        out_specs=(vmem,) * count,
        scratch_shapes=[
            pltpu.VMEM((shards * SHARD, HD), jnp.bfloat16),
            pltpu.VMEM((2, ROWS, HD), jnp.bfloat16),
            pltpu.VMEM((2, 8, ROWS), jnp.float32),
            pltpu.VMEM((2, ACC, ROWS), jnp.float32),
            pltpu.VMEM((int_rows, HD), jnp.int32),
            pltpu.SMEM((int_rows, HD), jnp.int32),
            pltpu.SMEM((2 * shards + 8,), jnp.int32),
            pltpu.SemaphoreType.DMA((len(pieces),)),
            pltpu.SemaphoreType.DMA,
        ],
        compiler_params=pltpu.CompilerParams(vmem_limit_bytes=VMEM_BYTES),
        cost_estimate=pl.CostEstimate(flops=pairs * HD * 4, bytes_accessed=8 << 20, transcendentals=pairs),
        name="attend",
    )(*args)


def combine_kernel(own_ref, one_ref, two_ref, three_ref, out_ref):
    for half in range(2):
        for h in range(HEADS):
            span = slice(half * ROWS + h * RUN, half * ROWS + (h + 1) * RUN)
            parts = [(own_ref[0:HD, span], own_ref[HD : HD + 1, span], own_ref[HD + 8 : HD + 9, span])]
            for ref in (one_ref, two_ref, three_ref):
                tail = ref[HD:ACC, span].astype(jnp.float32)
                parts.append(
                    (
                        ref[0:HD, span].astype(jnp.float32),
                        tail[0:1] + tail[1:2] + tail[2:3],
                        tail[3:4] + tail[4:5] + tail[5:6],
                    )
                )
            top = functools.reduce(jnp.maximum, [p[2] for p in parts])
            factors = [jnp.exp2(p[2] - top) for p in parts]
            numer = sum(p[0] * f for p, f in zip(parts, factors))
            total = sum(p[1] * f for p, f in zip(parts, factors))
            out_ref[half * RUN : (half + 1) * RUN, h * HD : (h + 1) * HD] = (
                (numer / total).T.astype(jnp.bfloat16)
            )


def combine(own, others):
    return pl.pallas_call(
        combine_kernel,
        out_shape=jax.ShapeDtypeStruct((2 * RUN, ROWS), jnp.bfloat16),
        in_specs=[pl.BlockSpec(memory_space=pltpu.VMEM)] * 4,
        out_specs=pl.BlockSpec(memory_space=pltpu.VMEM),
        compiler_params=pltpu.CompilerParams(vmem_limit_bytes=VMEM_BYTES),
        name="combine",
    )(own, *others)


def place_of(x, y, z, core):
    return ((x // 2) * 2 + core) * 32 + (y * 4 + z) * 2 + x % 2


def swap(array, flips):
    pairs = []
    for x in range(4):
        for y in range(4):
            for z in range(4):
                for core in range(2):
                    dx, dy, dz, dc = flips(core)
                    pairs.append((place_of(x, y, z, core), place_of(x ^ dx, y ^ dy, z ^ dz, core ^ dc)))
    return lax.ppermute(array, AXES, pairs)


def ring_x(array, step):
    return swap(array, lambda core: (step, 0, 0, 0))


def ring_first(array, step):
    return swap(array, lambda core: (0, step, 0, 0) if core else (0, 0, step, 0))


def ring_second(array, step):
    return swap(array, lambda core: (0, 0, step, 0) if core else (0, step, 0, 0))


def cores(array):
    return swap(array, lambda core: (0, 0, 0, 1))


def body(queries, keys, values, positions):
    shard = pack_kv(positions, keys, values)
    near = [ring_first(shard, s) for s in (1, 3, 2)]
    packed, acc0 = pack_q(queries, shard)
    near, packed, acc0 = lax.optimization_barrier((near, packed, acc0))
    line = jnp.concatenate([shard] + near, axis=0)
    q1, q3 = ring_x(packed, 1), ring_x(packed, 3)
    far1, far3 = ring_second(line, 1), ring_second(line, 3)
    far2 = ring_second(line, 2)
    line_x = cores(line)
    far1, far3, q1, q3, line_x = lax.optimization_barrier((far1, far3, q1, q3, line_x))
    first = [line, line_x, far1, far3, cores(far1), cores(far3)]
    (acc1,) = attend([q1], first, final=False)
    q2 = ring_x(packed, 2)
    last = [far2, cores(far2)]
    (part1,) = attend([q1], last, first, acc=[acc1])
    back1 = ring_x(part1, 1)
    (part3,) = attend([q3], first + last)
    back3 = ring_x(part3, 3)
    (part2,) = attend([q2], first + last)
    back2 = ring_x(part2, 2)
    (mine,) = attend([packed], first + last, base=acc0)
    return combine(mine, (back1, back3, back2))


def solution(mesh):
    return jax.shard_map(
        body,
        mesh=mesh,
        in_specs=(P(AXES, None), P(AXES, None), P(AXES, None), P(AXES)),
        out_specs=P(AXES, None),
        check_vma=False,
    )
```

```python
import functools
import math

import jax
import jax.numpy as jnp
from jax import lax
from jax.experimental import pallas as pl
from jax.experimental.pallas import tpu as pltpu
from jax.sharding import PartitionSpec as P

AXES = ("outer", "inner")
RUN = 128
HD = 128
HEADS = 8
ROWS = RUN * HEADS
SHARD = 4 * RUN + 16
QROWS = 2 * RUN + 16
ACC = HD + 16
GROUP = 8
COEF = HD**-0.5 * math.log2(math.e)
NEG = -1e30
LIMIT = 2.0**100
VMEM_BYTES = 22 * 2**20


def dot(a, b, ca, cb):
    return lax.dot_general(a, b, (((ca,), (cb,)), ((), ())), preferred_element_type=jnp.float32)


def split3(x):
    hi = x.astype(jnp.bfloat16)
    rest = x - hi.astype(jnp.float32)
    mid = rest.astype(jnp.bfloat16)
    low = (rest - mid.astype(jnp.float32)).astype(jnp.bfloat16)
    return hi, mid, low


def stack_rows(rows, width):
    at = lax.broadcasted_iota(jnp.int32, (16, width), 0)
    tile = jnp.zeros((16, width), jnp.float32)
    for i, row in enumerate(rows):
        tile = jnp.where(at == i, row.astype(jnp.float32), tile)
    return tile.astype(jnp.bfloat16)


def pack_kv_kernel(pos_ref, key_ref, value_ref, out_ref):
    out_ref[0 : 2 * RUN, :] = key_ref[...]
    for half in range(2):
        v = value_ref[half * RUN : (half + 1) * RUN, :].astype(jnp.float32)
        out_ref[(2 + half) * RUN : (3 + half) * RUN, :] = v.T.astype(jnp.bfloat16)
    block = (pos_ref[0] // RUN).astype(jnp.float32)
    out_ref[4 * RUN : SHARD, :] = jnp.full((16, HD), block, jnp.float32).astype(jnp.bfloat16)


def pack_kv(positions, keys, values):
    return pl.pallas_call(
        pack_kv_kernel,
        out_shape=jax.ShapeDtypeStruct((SHARD, HD), jnp.bfloat16),
        in_specs=[
            pl.BlockSpec(memory_space=pltpu.SMEM),
            pl.BlockSpec(memory_space=pltpu.VMEM),
            pl.BlockSpec(memory_space=pltpu.VMEM),
        ],
        out_specs=pl.BlockSpec(memory_space=pltpu.VMEM),
        name="pack_kv",
    )(positions, keys, values)


def query_tile(ref, half):
    rows = slice(half * RUN, (half + 1) * RUN)
    return jnp.concatenate([ref[rows, h * HD : (h + 1) * HD] for h in range(HEADS)], axis=0)


def pack_q_kernel(query_ref, shard_ref, out_ref, acc_ref):
    out_ref[0 : 2 * RUN, :] = query_ref[...]
    shifts = []
    key_at = lax.broadcasted_iota(jnp.int32, (RUN, ROWS), 0)
    row_at = lax.broadcasted_iota(jnp.int32, (RUN, ROWS), 1) % RUN
    ones = jnp.ones((16, RUN), jnp.bfloat16)
    for half in range(2):
        scores = dot(shard_ref[half * RUN : (half + 1) * RUN, :], query_tile(query_ref, half), 1, 1)
        scores = jnp.where(key_at <= row_at, scores * COEF, NEG)
        shift = jnp.max(scores, axis=0, keepdims=True)
        weights = jnp.exp2(scores - shift).astype(jnp.bfloat16)
        vt = jnp.concatenate([shard_ref[(2 + half) * RUN : (3 + half) * RUN, :], ones], axis=0)
        acc_ref[:, half * ROWS : (half + 1) * ROWS] = dot(vt, weights, 1, 0)
        shifts.append(shift)
    block = jnp.concatenate([shard_ref[4 * RUN : 4 * RUN + 1, :]] * HEADS, axis=1)
    out_ref[2 * RUN : QROWS, :] = stack_rows(split3(shifts[0]) + split3(shifts[1]) + (block,), ROWS)


def pack_q(queries, shard):
    return pl.pallas_call(
        pack_q_kernel,
        out_shape=(
            jax.ShapeDtypeStruct((QROWS, ROWS), jnp.bfloat16),
            jax.ShapeDtypeStruct((ACC, 2 * ROWS), jnp.float32),
        ),
        in_specs=[pl.BlockSpec(memory_space=pltpu.VMEM)] * 2,
        out_specs=(pl.BlockSpec(memory_space=pltpu.VMEM),) * 2,
        compiler_params=pltpu.CompilerParams(vmem_limit_bytes=VMEM_BYTES),
        name="pack_q",
    )(queries, shard)


def attend_kernel(count, sizes, old, have, base, final, keep, given, *refs):
    q_refs = refs[:count]
    at = count
    piece_refs = () if given else refs[at : at + len(sizes)]
    at += len(piece_refs)
    if given:
        kv_ref, numbers = refs[at : at + 2]
        at += 2
    in_refs = refs[at : at + count] if have else None
    at += count if have else 0
    base_ref = refs[at] if base else None
    at += 1 if base else 0
    out_refs = refs[at : at + count]
    at += count
    if keep:
        kv_ref, numbers = refs[at : at + 2]
        at += 2
    elif not given:
        kv_ref, numbers = refs[at : at + 2]
        at += 2
    q_buf, m_buf, acc_ref, tasks = refs[at : at + 4]
    ints, blocks, sems, sem = (None,) * 4 if given else refs[at + 4 :]
    starts = [sum(sizes[:i]) for i in range(len(sizes) + 1)]
    shards = starts[-1]

    def piece_copy(i):
        there = kv_ref.at[pl.ds(starts[i] * SHARD, sizes[i] * SHARD), :]
        return pltpu.make_async_copy(piece_refs[i], there, sems.at[i])

    def read_blocks(first, last):
        for i in range(first, last):
            row = kv_ref[i * SHARD + 4 * RUN : i * SHARD + SHARD, :].astype(jnp.float32)[0:1]
            ints[i : i + 1, :] = row.astype(jnp.int32)
        copy = pltpu.make_async_copy(ints, blocks, sem)
        copy.start()
        copy.wait()
        for i in range(first, last):
            numbers[i] = blocks[i, 0]

    if not given:
        for i in range(old, len(sizes)):
            piece_copy(i).start()

    def key_block(task):
        shard = task // 2
        start = pl.multiple_of(shard * SHARD + (task - 2 * shard) * RUN, 16)
        return kv_ref[pl.ds(start, RUN), :]

    def value_block(task):
        shard = task // 2
        start = pl.multiple_of(shard * SHARD + (2 + task - 2 * shard) * RUN, 16)
        return kv_ref[pl.ds(start, RUN), :]

    def list_tasks(here, first, last):
        total = 2 * (last - first)

        def place(i, ends):
            low, high = ends
            block = numbers[i]
            tasks[high] = 2 * i
            high = high - 1
            later = block > here
            tasks[jnp.where(later, high, total)] = 2 * i + 1
            high = high - later.astype(jnp.int32)
            earlier = block < here
            tasks[jnp.where(earlier, low, total)] = 2 * i
            low = low + earlier.astype(jnp.int32)
            return low, high

        for i in range(total):
            tasks[i] = 2 * first
        low_end, high_end = lax.fori_loop(first, last, place, (jnp.int32(0), jnp.int32(total - 1)))
        return low_end, high_end + 1

    ones = jnp.ones((16, GROUP * RUN), jnp.bfloat16)

    for j in range(count):
        q_ref = q_refs[j]
        tail = q_ref[2 * RUN : QROWS, :].astype(jnp.float32)
        for half in range(2):
            span = slice(half * ROWS, (half + 1) * ROWS)
            q_buf[half] = query_tile(q_ref, half)
            m_buf[half] = jnp.broadcast_to(
                tail[3 * half : 3 * half + 1]
                + tail[3 * half + 1 : 3 * half + 2]
                + tail[3 * half + 2 : 3 * half + 3],
                (8, ROWS),
            )
            if have:
                acc_ref[half] = in_refs[j][:, span]
            elif base:
                acc_ref[half] = base_ref[:, span]
            else:
                acc_ref[half] = jnp.zeros((ACC, ROWS), jnp.float32)
        here = jnp.max(tail[6:7, 0:HD]).astype(jnp.int32)
        if j == 0 and not given:
            for i in range(old, len(sizes)):
                piece_copy(i).wait()
            read_blocks(starts[old], shards)
        low_end, high_start = list_tasks(here, starts[old], shards)

        def pure(first, half):
            query = q_buf[half]
            shift = m_buf[half][0:1]
            parts = []
            for b in range(0, GROUP, 2):
                keys = jnp.concatenate([key_block(tasks[first + b]), key_block(tasks[first + b + 1])], axis=0)
                parts.append(jnp.exp2(dot(keys, query, 1, 1) * COEF - shift).astype(jnp.bfloat16))
            weights = jnp.concatenate(parts, axis=0)
            vt = jnp.concatenate([value_block(tasks[first + b]) for b in range(GROUP)], axis=1)
            vt = jnp.concatenate([vt, ones], axis=0)
            acc_ref[half] += dot(vt, weights, 1, 0)

        def mixed(first):
            parts = []
            for b in range(GROUP):
                half = (first + b >= high_start).astype(jnp.int32)
                scores = dot(key_block(tasks[first + b]), q_buf[half], 1, 1)
                parts.append(jnp.exp2(scores * COEF - m_buf[half][0:1]).astype(jnp.bfloat16))
            weights = jnp.concatenate(parts, axis=0)
            vt = jnp.concatenate([value_block(tasks[first + b]) for b in range(GROUP)], axis=1)
            vt = jnp.concatenate([vt, ones], axis=0)
            index = first + lax.broadcasted_iota(jnp.int32, (1, GROUP * RUN), 1) // RUN
            zero = jnp.zeros((), jnp.bfloat16)
            acc_ref[0] += dot(jnp.where(index < low_end, vt, zero), weights, 1, 0)
            acc_ref[1] += dot(jnp.where(index >= high_start, vt, zero), weights, 1, 0)

        @pl.loop(0, 2 * (shards - starts[old]) // GROUP)
        def _(g):
            first = g * GROUP
            is_low = first + GROUP <= low_end
            is_high = first >= high_start

            @pl.when(jnp.logical_or(is_low, is_high))
            def _():
                pure(first, is_high.astype(jnp.int32))

            @pl.when(jnp.logical_not(jnp.logical_or(is_low, is_high)))
            def _():
                mixed(first)

        if not final:
            for half in range(2):
                out_refs[j][:, half * ROWS : (half + 1) * ROWS] = acc_ref[half]
            continue

        sums = jnp.maximum(acc_ref[0][HD : HD + 8], acc_ref[1][HD : HD + 8])
        fine = jnp.min(jnp.where(sums < LIMIT, 1.0, 0.0)) > 0.5

        @pl.when(jnp.logical_not(fine))
        def _():
            for i in range(old):
                piece_copy(i).start()
            for i in range(old):
                piece_copy(i).wait()
            if old:
                read_blocks(0, starts[old])
            low_all, high_all = list_tasks(here, 0, shards)
            for half in range(2):
                if base:
                    acc_ref[half] = base_ref[:, half * ROWS : (half + 1) * ROWS]
                else:
                    acc_ref[half] = jnp.zeros((ACC, ROWS), jnp.float32)

            @pl.loop(0, 2 * shards)
            def _(t):
                @pl.when(jnp.logical_or(t < low_all, t >= high_all))
                def _():
                    half = (t >= high_all).astype(jnp.int32)
                    scores = dot(key_block(tasks[t]), q_buf[half], 1, 1) * COEF
                    before = m_buf[half][0:1]
                    new = jnp.maximum(before, jnp.max(scores, axis=0, keepdims=True))
                    weights = jnp.exp2(scores - new).astype(jnp.bfloat16)
                    vt = jnp.concatenate([value_block(tasks[t]), ones[:, :RUN]], axis=0)
                    acc_ref[half] = acc_ref[half] * jnp.exp2(before - new) + dot(vt, weights, 1, 0)
                    m_buf[half] = jnp.broadcast_to(new, (8, ROWS))

        for half in range(2):
            span = slice(half * ROWS, (half + 1) * ROWS)
            if base:
                out_refs[j][0 : HD + 8, span] = acc_ref[half][0 : HD + 8]
                out_refs[j][HD + 8 : ACC, span] = m_buf[half]
            else:
                acc = acc_ref[half]
                out_refs[j][0:HD, span] = acc[0:HD].astype(jnp.bfloat16)
                out_refs[j][HD:ACC, span] = stack_rows(
                    split3(acc[HD : HD + 1]) + split3(m_buf[half][0:1]), ROWS
                )


def attend(q_list, new=(), old=(), acc=None, base=None, final=True, keep=False, given=None):
    count = len(q_list)
    pieces = (tuple(old) if final else ()) + tuple(new)
    skip = len(old) if final else 0
    sizes = tuple(p.shape[0] // SHARD for p in pieces) if given is None else (given[0].shape[0] // SHARD,)
    shards = sum(sizes)
    int_rows = -(-shards // 8) * 8
    vmem, smem = pl.BlockSpec(memory_space=pltpu.VMEM), pl.BlockSpec(memory_space=pltpu.SMEM)
    args = list(q_list) + list(pieces)
    in_specs = [vmem] * count + [pl.BlockSpec(memory_space=pl.ANY)] * len(pieces)
    if given is not None:
        args += given
        in_specs += [vmem, smem]
    if acc is not None:
        args += acc
        in_specs += [vmem] * count
    if base is not None:
        args.append(base)
        in_specs.append(vmem)
    out = jax.ShapeDtypeStruct((ACC, 2 * ROWS), jnp.bfloat16 if final and base is None else jnp.float32)
    outs, out_specs = [out] * count, [vmem] * count
    scratch = []
    if keep:
        outs += [
            jax.ShapeDtypeStruct((shards * SHARD, HD), jnp.bfloat16),
            jax.ShapeDtypeStruct((int_rows,), jnp.int32),
        ]
        out_specs += [vmem, smem]
    elif given is None:
        scratch += [pltpu.VMEM((shards * SHARD, HD), jnp.bfloat16), pltpu.SMEM((int_rows,), jnp.int32)]
    scratch += [
        pltpu.VMEM((2, ROWS, HD), jnp.bfloat16),
        pltpu.VMEM((2, 8, ROWS), jnp.float32),
        pltpu.VMEM((2, ACC, ROWS), jnp.float32),
        pltpu.SMEM((2 * shards + 8,), jnp.int32),
    ]
    if given is None:
        scratch += [
            pltpu.VMEM((int_rows, HD), jnp.int32),
            pltpu.SMEM((int_rows, HD), jnp.int32),
            pltpu.SemaphoreType.DMA((len(pieces),)),
            pltpu.SemaphoreType.DMA,
        ]
    pairs = count * 2 * sum(sizes[skip:]) * RUN * ROWS
    flags = (count, sizes, skip, acc is not None, base is not None, final, keep, given is not None)
    return pl.pallas_call(
        functools.partial(attend_kernel, *flags),
        out_shape=outs,
        in_specs=in_specs,
        out_specs=out_specs,
        scratch_shapes=scratch,
        compiler_params=pltpu.CompilerParams(vmem_limit_bytes=VMEM_BYTES),
        cost_estimate=pl.CostEstimate(flops=pairs * HD * 4, bytes_accessed=8 << 20, transcendentals=pairs),
        name="attend",
    )(*args)


def combine_kernel(own_ref, one_ref, two_ref, three_ref, out_ref):
    for half in range(2):
        for h in range(HEADS):
            span = slice(half * ROWS + h * RUN, half * ROWS + (h + 1) * RUN)
            parts = [(own_ref[0:HD, span], own_ref[HD : HD + 1, span], own_ref[HD + 8 : HD + 9, span])]
            for ref in (one_ref, two_ref, three_ref):
                tail = ref[HD:ACC, span].astype(jnp.float32)
                parts.append(
                    (
                        ref[0:HD, span].astype(jnp.float32),
                        tail[0:1] + tail[1:2] + tail[2:3],
                        tail[3:4] + tail[4:5] + tail[5:6],
                    )
                )
            top = functools.reduce(jnp.maximum, [p[2] for p in parts])
            factors = [jnp.exp2(p[2] - top) for p in parts]
            numer = sum(p[0] * f for p, f in zip(parts, factors))
            total = sum(p[1] * f for p, f in zip(parts, factors))
            out_ref[half * RUN : (half + 1) * RUN, h * HD : (h + 1) * HD] = (
                (numer / total).T.astype(jnp.bfloat16)
            )


def combine(own, others):
    return pl.pallas_call(
        combine_kernel,
        out_shape=jax.ShapeDtypeStruct((2 * RUN, ROWS), jnp.bfloat16),
        in_specs=[pl.BlockSpec(memory_space=pltpu.VMEM)] * 4,
        out_specs=pl.BlockSpec(memory_space=pltpu.VMEM),
        compiler_params=pltpu.CompilerParams(vmem_limit_bytes=VMEM_BYTES),
        name="combine",
    )(own, *others)


def place_of(x, y, z, core):
    return ((x // 2) * 2 + core) * 32 + (y * 4 + z) * 2 + x % 2


def swap(array, flips):
    pairs = []
    for x in range(4):
        for y in range(4):
            for z in range(4):
                for core in range(2):
                    dx, dy, dz, dc = flips(core)
                    pairs.append((place_of(x, y, z, core), place_of(x ^ dx, y ^ dy, z ^ dz, core ^ dc)))
    return lax.ppermute(array, AXES, pairs)


def ring_x(array, step):
    return swap(array, lambda core: (step, 0, 0, 0))


def ring_first(array, step):
    return swap(array, lambda core: (0, step, 0, 0) if core else (0, 0, step, 0))


def ring_second(array, step):
    return swap(array, lambda core: (0, 0, step, 0) if core else (0, step, 0, 0))


def cores(array):
    return swap(array, lambda core: (0, 0, 0, 1))


def body(queries, keys, values, positions):
    shard = pack_kv(positions, keys, values)
    near = [ring_first(shard, s) for s in (1, 3, 2)]
    packed, acc0 = pack_q(queries, shard)
    near, packed, acc0 = lax.optimization_barrier((near, packed, acc0))
    line = jnp.concatenate([shard] + near, axis=0)
    q1, q3 = ring_x(packed, 1), ring_x(packed, 3)
    far1, far3 = ring_second(line, 1), ring_second(line, 3)
    far2 = ring_second(line, 2)
    line_x = cores(line)
    far1, far3, q1, q3, line_x = lax.optimization_barrier((far1, far3, q1, q3, line_x))
    first = [line, line_x, far1, far3, cores(far1), cores(far3)]
    (acc1,) = attend([q1], first, final=False)
    q2 = ring_x(packed, 2)
    last = [far2, cores(far2)]
    (part1,) = attend([q1], last, first, acc=[acc1])
    q3, part1 = lax.optimization_barrier((q3, part1))
    back1 = ring_x(part1, 1)
    part3, *whole = attend([q3], first + last, keep=True)
    q2, part3 = lax.optimization_barrier((q2, part3))
    back3 = ring_x(part3, 3)
    (part2,) = attend([q2], given=whole)
    packed, part2 = lax.optimization_barrier((packed, part2))
    back2 = ring_x(part2, 2)
    (mine,) = attend([packed], given=whole, base=acc0)
    return combine(mine, (back1, back3, back2))


def solution(mesh):
    return jax.shard_map(
        body,
        mesh=mesh,
        in_specs=(P(AXES, None), P(AXES, None), P(AXES, None), P(AXES)),
        out_specs=P(AXES, None),
        check_vma=False,
    )
```

```python
import functools
import math

import jax
import jax.numpy as jnp
from jax import lax
from jax.experimental import pallas as pl
from jax.experimental.pallas import tpu as pltpu
from jax.sharding import PartitionSpec as P

AXES = ("outer", "inner")
RUN = 128
HD = 128
HEADS = 8
ROWS = RUN * HEADS
SHARD = 4 * RUN + 16
QROWS = 2 * RUN + 16
ACC = HD + 16
COEF = HD**-0.5 * math.log2(math.e)
NEG = -1e30
LIMIT = 2.0**100
VMEM_BYTES = 22 * 2**20


def dot(a, b, ca, cb):
    return lax.dot_general(a, b, (((ca,), (cb,)), ((), ())), preferred_element_type=jnp.float32)


def split3(x):
    hi = x.astype(jnp.bfloat16)
    rest = x - hi.astype(jnp.float32)
    mid = rest.astype(jnp.bfloat16)
    low = (rest - mid.astype(jnp.float32)).astype(jnp.bfloat16)
    return hi, mid, low


def stack_rows(rows, width):
    at = lax.broadcasted_iota(jnp.int32, (16, width), 0)
    tile = jnp.zeros((16, width), jnp.float32)
    for i, row in enumerate(rows):
        tile = jnp.where(at == i, row.astype(jnp.float32), tile)
    return tile.astype(jnp.bfloat16)


def pack_kv_kernel(pos_ref, key_ref, value_ref, out_ref):
    out_ref[0 : 2 * RUN, :] = key_ref[...]
    for half in range(2):
        v = value_ref[half * RUN : (half + 1) * RUN, :].astype(jnp.float32)
        out_ref[(2 + half) * RUN : (3 + half) * RUN, :] = v.T.astype(jnp.bfloat16)
    block = (pos_ref[0] // RUN).astype(jnp.float32)
    out_ref[4 * RUN : SHARD, :] = jnp.full((16, HD), block, jnp.float32).astype(jnp.bfloat16)


def pack_kv(positions, keys, values):
    return pl.pallas_call(
        pack_kv_kernel,
        out_shape=jax.ShapeDtypeStruct((SHARD, HD), jnp.bfloat16),
        in_specs=[
            pl.BlockSpec(memory_space=pltpu.SMEM),
            pl.BlockSpec(memory_space=pltpu.VMEM),
            pl.BlockSpec(memory_space=pltpu.VMEM),
        ],
        out_specs=pl.BlockSpec(memory_space=pltpu.VMEM),
        name="pack_kv",
    )(positions, keys, values)


def query_tile(ref, half):
    rows = slice(half * RUN, (half + 1) * RUN)
    return jnp.concatenate([ref[rows, h * HD : (h + 1) * HD] for h in range(HEADS)], axis=0)


def pack_q_kernel(query_ref, shard_ref, out_ref, acc_ref):
    out_ref[0 : 2 * RUN, :] = query_ref[...]
    shifts = []
    key_at = lax.broadcasted_iota(jnp.int32, (RUN, ROWS), 0)
    row_at = lax.broadcasted_iota(jnp.int32, (RUN, ROWS), 1) % RUN
    ones = jnp.ones((16, RUN), jnp.bfloat16)
    for half in range(2):
        scores = dot(shard_ref[half * RUN : (half + 1) * RUN, :], query_tile(query_ref, half), 1, 1)
        scores = jnp.where(key_at <= row_at, scores * COEF, NEG)
        shift = jnp.max(scores, axis=0, keepdims=True)
        weights = jnp.exp2(scores - shift).astype(jnp.bfloat16)
        vt = jnp.concatenate([shard_ref[(2 + half) * RUN : (3 + half) * RUN, :], ones], axis=0)
        acc_ref[:, half * ROWS : (half + 1) * ROWS] = dot(vt, weights, 1, 0)
        shifts.append(shift)
    block = jnp.concatenate([shard_ref[4 * RUN : 4 * RUN + 1, :]] * HEADS, axis=1)
    out_ref[2 * RUN : QROWS, :] = stack_rows(split3(shifts[0]) + split3(shifts[1]) + (block,), ROWS)


def pack_q(queries, shard):
    return pl.pallas_call(
        pack_q_kernel,
        out_shape=(
            jax.ShapeDtypeStruct((QROWS, ROWS), jnp.bfloat16),
            jax.ShapeDtypeStruct((ACC, 2 * ROWS), jnp.float32),
        ),
        in_specs=[pl.BlockSpec(memory_space=pltpu.VMEM)] * 2,
        out_specs=(pl.BlockSpec(memory_space=pltpu.VMEM),) * 2,
        compiler_params=pltpu.CompilerParams(vmem_limit_bytes=VMEM_BYTES),
        name="pack_q",
    )(queries, shard)


def attend_kernel(count, sizes, old, done, only, have, base, final, keep, given, *refs):
    halves = (0, 1) if only is None else (only,)
    q_refs = refs[:count]
    at = count
    piece_refs = () if given else refs[at : at + len(sizes)]
    at += len(piece_refs)
    if given:
        kv_ref, numbers = refs[at : at + 2]
        at += 2
    in_refs = refs[at : at + count] if have else None
    at += count if have else 0
    base_ref = refs[at] if base else None
    at += 1 if base else 0
    out_refs = refs[at : at + count]
    at += count
    if keep:
        kv_ref, numbers = refs[at : at + 2]
        at += 2
    elif not given:
        kv_ref, numbers = refs[at : at + 2]
        at += 2
    q_buf, m_buf, acc_ref, tasks = refs[at : at + 4]
    ints, blocks, sems, sem = (None,) * 4 if given else refs[at + 4 :]
    starts = [sum(sizes[:i]) for i in range(len(sizes) + 1)]
    shards = starts[-1]
    group = 16 if shards - done >= 24 and given and only is None else 8

    def piece_copy(i):
        there = kv_ref.at[pl.ds(starts[i] * SHARD, sizes[i] * SHARD), :]
        return pltpu.make_async_copy(piece_refs[i], there, sems.at[i])

    def read_blocks(first, last):
        for i in range(first, last):
            row = kv_ref[i * SHARD + 4 * RUN : i * SHARD + SHARD, :].astype(jnp.float32)[0:1]
            ints[i : i + 1, :] = row.astype(jnp.int32)
        copy = pltpu.make_async_copy(ints, blocks, sem)
        copy.start()
        copy.wait()
        for i in range(first, last):
            numbers[i] = blocks[i, 0]

    if not given:
        for i in list(range(old, len(sizes))) + (list(range(old)) if keep else []):
            piece_copy(i).start()

    def key_block(task):
        shard = task // 2
        start = pl.multiple_of(shard * SHARD + (task - 2 * shard) * RUN, 16)
        return kv_ref[pl.ds(start, RUN), :]

    def value_block(task):
        shard = task // 2
        start = pl.multiple_of(shard * SHARD + (2 + task - 2 * shard) * RUN, 16)
        return kv_ref[pl.ds(start, RUN), :]

    def list_tasks(here, first, last):
        total = 2 * (last - first)

        def place(i, ends):
            low, high = ends
            block = numbers[i]
            tasks[high] = 2 * i
            high = high - 1
            later = block > here
            tasks[jnp.where(later, high, total)] = 2 * i + 1
            high = high - later.astype(jnp.int32)
            earlier = block < here
            tasks[jnp.where(earlier, low, total)] = 2 * i
            low = low + earlier.astype(jnp.int32)
            return low, high

        for i in range(total):
            tasks[i] = 2 * first
        low_end, high_end = lax.fori_loop(first, last, place, (jnp.int32(0), jnp.int32(total - 1)))
        return low_end, high_end + 1

    ones = jnp.ones((16, group * RUN), jnp.bfloat16)

    for j in range(count):
        q_ref = q_refs[j]
        tail = q_ref[2 * RUN : QROWS, :].astype(jnp.float32)
        for half in halves:
            span = slice(half * ROWS, (half + 1) * ROWS)
            q_buf[half] = query_tile(q_ref, half)
            m_buf[half] = jnp.broadcast_to(
                tail[3 * half : 3 * half + 1]
                + tail[3 * half + 1 : 3 * half + 2]
                + tail[3 * half + 2 : 3 * half + 3],
                (8, ROWS),
            )
            if have:
                acc_ref[half] = in_refs[j][:, span]
            elif base:
                acc_ref[half] = base_ref[:, span]
            else:
                acc_ref[half] = jnp.zeros((ACC, ROWS), jnp.float32)
        here = jnp.max(tail[6:7, 0:HD]).astype(jnp.int32)
        if j == 0 and not given:
            for i in range(old, len(sizes)):
                piece_copy(i).wait()
            read_blocks(starts[old], shards)
        low_end, high_start = list_tasks(here, done, shards)

        def pure(first, half):
            query = q_buf[half]
            shift = m_buf[half][0:1]
            parts = []
            for b in range(0, group, 2):
                keys = jnp.concatenate([key_block(tasks[first + b]), key_block(tasks[first + b + 1])], axis=0)
                parts.append(jnp.exp2(dot(keys, query, 1, 1) * COEF - shift).astype(jnp.bfloat16))
            weights = jnp.concatenate(parts, axis=0)
            vt = jnp.concatenate([value_block(tasks[first + b]) for b in range(group)], axis=1)
            vt = jnp.concatenate([vt, ones], axis=0)
            acc_ref[half] += dot(vt, weights, 1, 0)

        def mixed(first):
            parts = []
            for b in range(group):
                half = (first + b >= high_start).astype(jnp.int32) if only is None else only
                scores = dot(key_block(tasks[first + b]), q_buf[half], 1, 1)
                parts.append(jnp.exp2(scores * COEF - m_buf[half][0:1]).astype(jnp.bfloat16))
            weights = jnp.concatenate(parts, axis=0)
            vt = jnp.concatenate([value_block(tasks[first + b]) for b in range(group)], axis=1)
            vt = jnp.concatenate([vt, ones], axis=0)
            index = first + lax.broadcasted_iota(jnp.int32, (1, group * RUN), 1) // RUN
            zero = jnp.zeros((), jnp.bfloat16)
            if 0 in halves:
                acc_ref[0] += dot(jnp.where(index < low_end, vt, zero), weights, 1, 0)
            if 1 in halves:
                acc_ref[1] += dot(jnp.where(index >= high_start, vt, zero), weights, 1, 0)

        steps = 2 * (shards - done) // group

        @pl.loop(high_start // group if only == 1 else 0, (low_end + group - 1) // group if only == 0 else steps)
        def _(g):
            first = g * group
            is_low = first + group <= low_end
            is_high = first >= high_start

            @pl.when(jnp.logical_or(is_low, is_high))
            def _():
                pure(first, is_high.astype(jnp.int32) if only is None else only)

            @pl.when(jnp.logical_not(jnp.logical_or(is_low, is_high)))
            def _():
                mixed(first)

        if keep and old:
            for i in range(old):
                piece_copy(i).wait()
            read_blocks(0, starts[old])

        if not final:
            for half in range(2):
                out_refs[j][:, half * ROWS : (half + 1) * ROWS] = acc_ref[half]
            continue

        sums = functools.reduce(jnp.maximum, [acc_ref[half][HD : HD + 8] for half in halves])
        fine = jnp.min(jnp.where(sums < LIMIT, 1.0, 0.0)) > 0.5

        @pl.when(jnp.logical_not(fine))
        def _():
            if old and not keep:
                for i in range(old):
                    piece_copy(i).start()
                for i in range(old):
                    piece_copy(i).wait()
                read_blocks(0, starts[old])
            low_all, high_all = list_tasks(here, 0, shards)
            for half in halves:
                if base:
                    acc_ref[half] = base_ref[:, half * ROWS : (half + 1) * ROWS]
                else:
                    acc_ref[half] = jnp.zeros((ACC, ROWS), jnp.float32)

            @pl.loop(0, 2 * shards)
            def _(t):
                in_low = jnp.logical_and(t < low_all, only != 1)
                in_high = jnp.logical_and(t >= high_all, only != 0)

                @pl.when(jnp.logical_or(in_low, in_high))
                def _():
                    half = (t >= high_all).astype(jnp.int32) if only is None else only
                    scores = dot(key_block(tasks[t]), q_buf[half], 1, 1) * COEF
                    before = m_buf[half][0:1]
                    new = jnp.maximum(before, jnp.max(scores, axis=0, keepdims=True))
                    weights = jnp.exp2(scores - new).astype(jnp.bfloat16)
                    vt = jnp.concatenate([value_block(tasks[t]), ones[:, :RUN]], axis=0)
                    acc_ref[half] = acc_ref[half] * jnp.exp2(before - new) + dot(vt, weights, 1, 0)
                    m_buf[half] = jnp.broadcast_to(new, (8, ROWS))

        for half in halves:
            span = slice(half * ROWS, (half + 1) * ROWS) if only is None else slice(0, ROWS)
            if base:
                out_refs[j][0 : HD + 8, span] = acc_ref[half][0 : HD + 8]
                out_refs[j][HD + 8 : ACC, span] = m_buf[half]
            else:
                acc = acc_ref[half]
                out_refs[j][0:HD, span] = acc[0:HD].astype(jnp.bfloat16)
                out_refs[j][HD:ACC, span] = stack_rows(
                    split3(acc[HD : HD + 1]) + split3(m_buf[half][0:1]), ROWS
                )


def attend(q_list, new=(), old=(), acc=None, base=None, final=True, keep=False, given=None, done=0, only=None):
    count = len(q_list)
    pieces = (tuple(old) if final else ()) + tuple(new)
    skip = len(old) if final else 0
    sizes = tuple(p.shape[0] // SHARD for p in pieces) if given is None else (given[0].shape[0] // SHARD,)
    shards = sum(sizes)
    done = done if given is not None else sum(sizes[:skip])
    int_rows = -(-shards // 8) * 8
    vmem, smem = pl.BlockSpec(memory_space=pltpu.VMEM), pl.BlockSpec(memory_space=pltpu.SMEM)
    args = list(q_list) + list(pieces)
    in_specs = [vmem] * count + [pl.BlockSpec(memory_space=pl.ANY)] * len(pieces)
    if given is not None:
        args += given
        in_specs += [vmem, smem]
    if acc is not None:
        args += acc
        in_specs += [vmem] * count
    if base is not None:
        args.append(base)
        in_specs.append(vmem)
    out = jax.ShapeDtypeStruct((ACC, (2 if only is None else 1) * ROWS), jnp.bfloat16 if final and base is None else jnp.float32)
    outs, out_specs = [out] * count, [vmem] * count
    scratch = []
    if keep:
        outs += [
            jax.ShapeDtypeStruct((shards * SHARD, HD), jnp.bfloat16),
            jax.ShapeDtypeStruct((int_rows,), jnp.int32),
        ]
        out_specs += [vmem, smem]
    elif given is None:
        scratch += [pltpu.VMEM((shards * SHARD, HD), jnp.bfloat16), pltpu.SMEM((int_rows,), jnp.int32)]
    scratch += [
        pltpu.VMEM((2, ROWS, HD), jnp.bfloat16),
        pltpu.VMEM((2, 8, ROWS), jnp.float32),
        pltpu.VMEM((2, ACC, ROWS), jnp.float32),
        pltpu.SMEM((2 * shards + 8,), jnp.int32),
    ]
    if given is None:
        scratch += [
            pltpu.VMEM((int_rows, HD), jnp.int32),
            pltpu.SMEM((int_rows, HD), jnp.int32),
            pltpu.SemaphoreType.DMA((len(pieces),)),
            pltpu.SemaphoreType.DMA,
        ]
    pairs = count * 2 * (shards - done) * RUN * ROWS
    flags = (count, sizes, skip, done, only, acc is not None, base is not None, final, keep, given is not None)
    return pl.pallas_call(
        functools.partial(attend_kernel, *flags),
        out_shape=outs,
        in_specs=in_specs,
        out_specs=out_specs,
        scratch_shapes=scratch,
        compiler_params=pltpu.CompilerParams(vmem_limit_bytes=VMEM_BYTES),
        cost_estimate=pl.CostEstimate(flops=pairs, bytes_accessed=1 << 20, transcendentals=0),
        name="attend",
    )(*args)


def combine_kernel(own_ref, one_ref, two_ref, low_ref, high_ref, out_ref):
    for half in range(2):
        for h in range(HEADS):
            span = slice(half * ROWS + h * RUN, half * ROWS + (h + 1) * RUN)
            parts = [(own_ref[0:HD, span], own_ref[HD : HD + 1, span], own_ref[HD + 8 : HD + 9, span])]
            within = slice(h * RUN, (h + 1) * RUN)
            for ref, at in ((one_ref, span), (two_ref, span), ((low_ref, high_ref)[half], within)):
                tail = ref[HD:ACC, at].astype(jnp.float32)
                parts.append(
                    (
                        ref[0:HD, at].astype(jnp.float32),
                        tail[0:1] + tail[1:2] + tail[2:3],
                        tail[3:4] + tail[4:5] + tail[5:6],
                    )
                )
            top = functools.reduce(jnp.maximum, [p[2] for p in parts])
            factors = [jnp.exp2(p[2] - top) for p in parts]
            numer = sum(p[0] * f for p, f in zip(parts, factors))
            total = sum(p[1] * f for p, f in zip(parts, factors))
            out_ref[half * RUN : (half + 1) * RUN, h * HD : (h + 1) * HD] = (
                (numer / total).T.astype(jnp.bfloat16)
            )


def combine(own, others):
    return pl.pallas_call(
        combine_kernel,
        out_shape=jax.ShapeDtypeStruct((2 * RUN, ROWS), jnp.bfloat16),
        in_specs=[pl.BlockSpec(memory_space=pltpu.VMEM)] * 5,
        out_specs=pl.BlockSpec(memory_space=pltpu.VMEM),
        compiler_params=pltpu.CompilerParams(vmem_limit_bytes=VMEM_BYTES),
        name="combine",
    )(own, *others)


def place_of(x, y, z, core):
    return ((x // 2) * 2 + core) * 32 + (y * 4 + z) * 2 + x % 2


def swap(array, flips):
    pairs = []
    for x in range(4):
        for y in range(4):
            for z in range(4):
                for core in range(2):
                    dx, dy, dz, dc = flips(core)
                    pairs.append((place_of(x, y, z, core), place_of(x ^ dx, y ^ dy, z ^ dz, core ^ dc)))
    return lax.ppermute(array, AXES, pairs)


def ring_x(array, step):
    return swap(array, lambda core: (step, 0, 0, 0))


def ring_first(array, step):
    return swap(array, lambda core: (0, step, 0, 0) if core else (0, 0, step, 0))


def ring_second(array, step):
    return swap(array, lambda core: (0, 0, step, 0) if core else (0, step, 0, 0))


def cores(array):
    return swap(array, lambda core: (0, 0, 0, 1))


def body(queries, keys, values, positions):
    shard = pack_kv(positions, keys, values)
    near = [ring_first(shard, s) for s in (1, 3, 2)]
    packed, acc0 = pack_q(queries, shard)
    near, packed, acc0 = lax.optimization_barrier((near, packed, acc0))
    line = jnp.concatenate([shard] + near, axis=0)
    q2 = ring_x(packed, 2)
    far1, far3 = ring_second(line, 1), ring_second(line, 3)
    line_x = cores(line)
    (acc_own,) = attend([packed], [line, line_x], base=acc0, final=False)
    far1, far3, q2, line_x, line, packed, acc_own = lax.optimization_barrier(
        (far1, far3, q2, line_x, line, packed, acc_own)
    )
    far2 = ring_second(line, 2)
    q1, q3 = ring_x(packed, 1), ring_x(packed, 3)
    first = [line, line_x, far1, far3, cores(far1), cores(far3)]
    (acc2,) = attend([q2], first, final=False)
    far2, acc2 = lax.optimization_barrier((far2, acc2))
    last = [far2, cores(far2)]
    part2, *whole = attend([q2], last, first, acc=[acc2], keep=True)
    q1, q3, part2 = lax.optimization_barrier((q1, q3, part2))
    back2 = ring_x(part2, 2)
    (part1,) = attend([q1], given=whole)
    q3, part1 = lax.optimization_barrier((q3, part1))
    back1 = ring_x(part1, 1)
    (low3,) = attend([q3], given=whole, only=0)
    q3, low3, back2 = lax.optimization_barrier((q3, low3, back2))
    back_low = ring_x(low3, 3)
    (high3,) = attend([q3], given=whole, only=1)
    packed, high3 = lax.optimization_barrier((packed, high3))
    back_high = ring_x(high3, 3)
    packed, back_low = lax.optimization_barrier((packed, back_low))
    (mine,) = attend([packed], given=whole, acc=[acc_own], base=acc0, done=8)
    return combine(mine, (back1, back2, back_low, back_high))


def solution(mesh):
    return jax.shard_map(
        body,
        mesh=mesh,
        in_specs=(P(AXES, None), P(AXES, None), P(AXES, None), P(AXES)),
        out_specs=P(AXES, None),
        check_vma=False,
    )
```

```python
import functools
import math

import jax
import jax.numpy as jnp
from jax import lax
from jax.experimental import pallas as pl
from jax.experimental.pallas import tpu as pltpu
from jax.sharding import PartitionSpec as P

AXES = ("outer", "inner")
RUN = 128
HD = 128
HEADS = 8
ROWS = RUN * HEADS
SHARD = 4 * RUN + 16
QROWS = 2 * RUN + 16
ACC = HD + 16
COEF = HD**-0.5 * math.log2(math.e)
NEG = -1e30
LIMIT = 2.0**100
VMEM_BYTES = 22 * 2**20


def dot(a, b, ca, cb):
    return lax.dot_general(a, b, (((ca,), (cb,)), ((), ())), preferred_element_type=jnp.float32)


def split3(x):
    hi = x.astype(jnp.bfloat16)
    rest = x - hi.astype(jnp.float32)
    mid = rest.astype(jnp.bfloat16)
    low = (rest - mid.astype(jnp.float32)).astype(jnp.bfloat16)
    return hi, mid, low


def stack_rows(rows, width):
    at = lax.broadcasted_iota(jnp.int32, (16, width), 0)
    tile = jnp.zeros((16, width), jnp.float32)
    for i, row in enumerate(rows):
        tile = jnp.where(at == i, row.astype(jnp.float32), tile)
    return tile.astype(jnp.bfloat16)


def pack_kv_kernel(pos_ref, key_ref, value_ref, out_ref):
    out_ref[0 : 2 * RUN, :] = key_ref[...]
    for half in range(2):
        v = value_ref[half * RUN : (half + 1) * RUN, :].astype(jnp.float32)
        out_ref[(2 + half) * RUN : (3 + half) * RUN, :] = v.T.astype(jnp.bfloat16)
    block = (pos_ref[0] // RUN).astype(jnp.float32)
    out_ref[4 * RUN : SHARD, :] = jnp.full((16, HD), block, jnp.float32).astype(jnp.bfloat16)


def pack_kv(positions, keys, values):
    return pl.pallas_call(
        pack_kv_kernel,
        out_shape=jax.ShapeDtypeStruct((SHARD, HD), jnp.bfloat16),
        in_specs=[
            pl.BlockSpec(memory_space=pltpu.SMEM),
            pl.BlockSpec(memory_space=pltpu.VMEM),
            pl.BlockSpec(memory_space=pltpu.VMEM),
        ],
        out_specs=pl.BlockSpec(memory_space=pltpu.VMEM),
        name="pack_kv",
    )(positions, keys, values)


def query_tile(ref, half):
    rows = slice(half * RUN, (half + 1) * RUN)
    return jnp.concatenate([ref[rows, h * HD : (h + 1) * HD] for h in range(HEADS)], axis=0)


def pack_q_kernel(query_ref, shard_ref, out_ref, acc_ref):
    out_ref[0 : 2 * RUN, :] = query_ref[...]
    shifts = []
    key_at = lax.broadcasted_iota(jnp.int32, (RUN, ROWS), 0)
    row_at = lax.broadcasted_iota(jnp.int32, (RUN, ROWS), 1) % RUN
    ones = jnp.ones((16, RUN), jnp.bfloat16)
    for half in range(2):
        scores = dot(shard_ref[half * RUN : (half + 1) * RUN, :], query_tile(query_ref, half), 1, 1)
        scores = jnp.where(key_at <= row_at, scores * COEF, NEG)
        shift = jnp.max(scores, axis=0, keepdims=True)
        weights = jnp.exp2(scores - shift).astype(jnp.bfloat16)
        vt = jnp.concatenate([shard_ref[(2 + half) * RUN : (3 + half) * RUN, :], ones], axis=0)
        acc_ref[:, half * ROWS : (half + 1) * ROWS] = dot(vt, weights, 1, 0)
        shifts.append(shift)
    block = jnp.concatenate([shard_ref[4 * RUN : 4 * RUN + 1, :]] * HEADS, axis=1)
    out_ref[2 * RUN : QROWS, :] = stack_rows(split3(shifts[0]) + split3(shifts[1]) + (block,), ROWS)


def pack_q(queries, shard):
    return pl.pallas_call(
        pack_q_kernel,
        out_shape=(
            jax.ShapeDtypeStruct((QROWS, ROWS), jnp.bfloat16),
            jax.ShapeDtypeStruct((ACC, 2 * ROWS), jnp.float32),
        ),
        in_specs=[pl.BlockSpec(memory_space=pltpu.VMEM)] * 2,
        out_specs=(pl.BlockSpec(memory_space=pltpu.VMEM),) * 2,
        compiler_params=pltpu.CompilerParams(vmem_limit_bytes=VMEM_BYTES),
        name="pack_q",
    )(queries, shard)


def attend_kernel(count, sizes, old, done, only, have, base, final, keep, given, *refs):
    whole_only = only
    q_refs = refs[:count]
    at = count
    piece_refs = () if given else refs[at : at + len(sizes)]
    at += len(piece_refs)
    if given:
        kv_ref, numbers = refs[at : at + 2]
        at += 2
    in_refs = refs[at : at + count] if have else None
    at += count if have else 0
    base_ref = refs[at] if base else None
    at += 1 if base else 0
    out_refs = refs[at : at + count]
    at += count
    if keep:
        kv_ref, numbers = refs[at : at + 2]
        at += 2
    elif not given:
        kv_ref, numbers = refs[at : at + 2]
        at += 2
    q_buf, m_buf, acc_ref, tasks = refs[at : at + 4]
    ints, blocks, sems, sem = (None,) * 4 if given else refs[at + 4 :]
    starts = [sum(sizes[:i]) for i in range(len(sizes) + 1)]
    shards = starts[-1]
    group = 16 if shards - done >= 24 and given and only[-1] != 1 else 8

    def piece_copy(i):
        there = kv_ref.at[pl.ds(starts[i] * SHARD, sizes[i] * SHARD), :]
        return pltpu.make_async_copy(piece_refs[i], there, sems.at[i])

    def read_blocks(first, last):
        for i in range(first, last):
            row = kv_ref[i * SHARD + 4 * RUN : i * SHARD + SHARD, :].astype(jnp.float32)[0:1]
            ints[i : i + 1, :] = row.astype(jnp.int32)
        copy = pltpu.make_async_copy(ints, blocks, sem)
        copy.start()
        copy.wait()
        for i in range(first, last):
            numbers[i] = blocks[i, 0]

    if not given:
        for i in list(range(old, len(sizes))) + (list(range(old)) if keep else []):
            piece_copy(i).start()

    def key_block(task):
        shard = task // 2
        start = pl.multiple_of(shard * SHARD + (task - 2 * shard) * RUN, 16)
        return kv_ref[pl.ds(start, RUN), :]

    def value_block(task):
        shard = task // 2
        start = pl.multiple_of(shard * SHARD + (2 + task - 2 * shard) * RUN, 16)
        return kv_ref[pl.ds(start, RUN), :]

    def list_tasks(here, first, last):
        total = 2 * (last - first)

        def place(i, ends):
            low, high = ends
            block = numbers[i]
            tasks[high] = 2 * i
            high = high - 1
            later = block > here
            tasks[jnp.where(later, high, total)] = 2 * i + 1
            high = high - later.astype(jnp.int32)
            earlier = block < here
            tasks[jnp.where(earlier, low, total)] = 2 * i
            low = low + earlier.astype(jnp.int32)
            return low, high

        for i in range(total):
            tasks[i] = 2 * first
        low_end, high_end = lax.fori_loop(first, last, place, (jnp.int32(0), jnp.int32(total - 1)))
        return low_end, high_end + 1

    ones = jnp.ones((16, group * RUN), jnp.bfloat16)

    for j in range(count):
        only = whole_only[j]
        halves = (0, 1) if only is None else (only,)
        q_ref = q_refs[j]
        tail = q_ref[2 * RUN : QROWS, :].astype(jnp.float32)
        for half in halves:
            span = slice(half * ROWS, (half + 1) * ROWS)
            q_buf[half] = query_tile(q_ref, half)
            m_buf[half] = jnp.broadcast_to(
                tail[3 * half : 3 * half + 1]
                + tail[3 * half + 1 : 3 * half + 2]
                + tail[3 * half + 2 : 3 * half + 3],
                (8, ROWS),
            )
            if have:
                acc_ref[half] = in_refs[j][:, span]
            elif base:
                acc_ref[half] = base_ref[:, span]
            else:
                acc_ref[half] = jnp.zeros((ACC, ROWS), jnp.float32)
        here = jnp.max(tail[6:7, 0:HD]).astype(jnp.int32)
        if j == 0 and not given:
            for i in range(old, len(sizes)):
                piece_copy(i).wait()
            read_blocks(starts[old], shards)
        low_end, high_start = list_tasks(here, done, shards)

        def pure(first, half):
            query = q_buf[half]
            shift = m_buf[half][0:1]
            parts = []
            for b in range(0, group, 2):
                keys = jnp.concatenate([key_block(tasks[first + b]), key_block(tasks[first + b + 1])], axis=0)
                parts.append(jnp.exp2(dot(keys, query, 1, 1) * COEF - shift).astype(jnp.bfloat16))
            weights = jnp.concatenate(parts, axis=0)
            vt = jnp.concatenate([value_block(tasks[first + b]) for b in range(group)], axis=1)
            vt = jnp.concatenate([vt, ones], axis=0)
            acc_ref[half] += dot(vt, weights, 1, 0)

        def mixed(first):
            parts = []
            for b in range(group):
                half = (first + b >= high_start).astype(jnp.int32) if only is None else only
                scores = dot(key_block(tasks[first + b]), q_buf[half], 1, 1)
                parts.append(jnp.exp2(scores * COEF - m_buf[half][0:1]).astype(jnp.bfloat16))
            weights = jnp.concatenate(parts, axis=0)
            vt = jnp.concatenate([value_block(tasks[first + b]) for b in range(group)], axis=1)
            vt = jnp.concatenate([vt, ones], axis=0)
            index = first + lax.broadcasted_iota(jnp.int32, (1, group * RUN), 1) // RUN
            zero = jnp.zeros((), jnp.bfloat16)
            if 0 in halves:
                acc_ref[0] += dot(jnp.where(index < low_end, vt, zero), weights, 1, 0)
            if 1 in halves:
                acc_ref[1] += dot(jnp.where(index >= high_start, vt, zero), weights, 1, 0)

        steps = 2 * (shards - done) // group

        @pl.loop(high_start // group if only == 1 else 0, (low_end + group - 1) // group if only == 0 else steps)
        def _(g):
            first = g * group
            is_low = first + group <= low_end
            is_high = first >= high_start

            @pl.when(jnp.logical_or(is_low, is_high))
            def _():
                pure(first, is_high.astype(jnp.int32) if only is None else only)

            @pl.when(jnp.logical_not(jnp.logical_or(is_low, is_high)))
            def _():
                mixed(first)

        if keep and old:
            for i in range(old):
                piece_copy(i).wait()
            read_blocks(0, starts[old])

        if not final:
            for half in range(2):
                out_refs[j][:, half * ROWS : (half + 1) * ROWS] = acc_ref[half]
            continue

        sums = functools.reduce(jnp.maximum, [acc_ref[half][HD : HD + 8] for half in halves])
        fine = jnp.min(jnp.where(sums < LIMIT, 1.0, 0.0)) > 0.5

        @pl.when(jnp.logical_not(fine))
        def _():
            if old and not keep:
                for i in range(old):
                    piece_copy(i).start()
                for i in range(old):
                    piece_copy(i).wait()
                read_blocks(0, starts[old])
            low_all, high_all = list_tasks(here, 0, shards)
            for half in halves:
                if base:
                    acc_ref[half] = base_ref[:, half * ROWS : (half + 1) * ROWS]
                else:
                    acc_ref[half] = jnp.zeros((ACC, ROWS), jnp.float32)

            @pl.loop(0, 2 * shards)
            def _(t):
                in_low = jnp.logical_and(t < low_all, only != 1)
                in_high = jnp.logical_and(t >= high_all, only != 0)

                @pl.when(jnp.logical_or(in_low, in_high))
                def _():
                    half = (t >= high_all).astype(jnp.int32) if only is None else only
                    scores = dot(key_block(tasks[t]), q_buf[half], 1, 1) * COEF
                    before = m_buf[half][0:1]
                    new = jnp.maximum(before, jnp.max(scores, axis=0, keepdims=True))
                    weights = jnp.exp2(scores - new).astype(jnp.bfloat16)
                    vt = jnp.concatenate([value_block(tasks[t]), ones[:, :RUN]], axis=0)
                    acc_ref[half] = acc_ref[half] * jnp.exp2(before - new) + dot(vt, weights, 1, 0)
                    m_buf[half] = jnp.broadcast_to(new, (8, ROWS))

        for half in halves:
            span = slice(half * ROWS, (half + 1) * ROWS) if only is None else slice(0, ROWS)
            if base:
                out_refs[j][0 : HD + 8, span] = acc_ref[half][0 : HD + 8]
                out_refs[j][HD + 8 : ACC, span] = m_buf[half]
            else:
                acc = acc_ref[half]
                out_refs[j][0:HD, span] = acc[0:HD].astype(jnp.bfloat16)
                out_refs[j][HD:ACC, span] = stack_rows(
                    split3(acc[HD : HD + 1]) + split3(m_buf[half][0:1]), ROWS
                )


def attend(q_list, new=(), old=(), acc=None, base=None, final=True, keep=False, given=None, done=0, only=None):
    only = only or (None,) * len(q_list)
    count = len(q_list)
    pieces = (tuple(old) if final else ()) + tuple(new)
    skip = len(old) if final else 0
    sizes = tuple(p.shape[0] // SHARD for p in pieces) if given is None else (given[0].shape[0] // SHARD,)
    shards = sum(sizes)
    done = done if given is not None else sum(sizes[:skip])
    int_rows = -(-shards // 8) * 8
    vmem, smem = pl.BlockSpec(memory_space=pltpu.VMEM), pl.BlockSpec(memory_space=pltpu.SMEM)
    args = list(q_list) + list(pieces)
    in_specs = [vmem] * count + [pl.BlockSpec(memory_space=pl.ANY)] * len(pieces)
    if given is not None:
        args += given
        in_specs += [vmem, smem]
    if acc is not None:
        args += acc
        in_specs += [vmem] * count
    if base is not None:
        args.append(base)
        in_specs.append(vmem)
    kind = jnp.bfloat16 if final and base is None else jnp.float32
    outs = [jax.ShapeDtypeStruct((ACC, (2 if run is None else 1) * ROWS), kind) for run in only]
    out_specs = [vmem] * count
    scratch = []
    if keep:
        outs += [
            jax.ShapeDtypeStruct((shards * SHARD, HD), jnp.bfloat16),
            jax.ShapeDtypeStruct((int_rows,), jnp.int32),
        ]
        out_specs += [vmem, smem]
    elif given is None:
        scratch += [pltpu.VMEM((shards * SHARD, HD), jnp.bfloat16), pltpu.SMEM((int_rows,), jnp.int32)]
    scratch += [
        pltpu.VMEM((2, ROWS, HD), jnp.bfloat16),
        pltpu.VMEM((2, 8, ROWS), jnp.float32),
        pltpu.VMEM((2, ACC, ROWS), jnp.float32),
        pltpu.SMEM((2 * shards + 8,), jnp.int32),
    ]
    if given is None:
        scratch += [
            pltpu.VMEM((int_rows, HD), jnp.int32),
            pltpu.SMEM((int_rows, HD), jnp.int32),
            pltpu.SemaphoreType.DMA((len(pieces),)),
            pltpu.SemaphoreType.DMA,
        ]
    pairs = count * 2 * (shards - done) * RUN * ROWS
    flags = (count, sizes, skip, done, only, acc is not None, base is not None, final, keep, given is not None)
    return pl.pallas_call(
        functools.partial(attend_kernel, *flags),
        out_shape=outs,
        in_specs=in_specs,
        out_specs=out_specs,
        scratch_shapes=scratch,
        compiler_params=pltpu.CompilerParams(vmem_limit_bytes=VMEM_BYTES),
        cost_estimate=pl.CostEstimate(flops=pairs, bytes_accessed=1 << 20, transcendentals=0),
        name="attend",
    )(*args)


def combine_kernel(own_ref, one_ref, two_ref, low_ref, high_ref, out_ref):
    for half in range(2):
        for h in range(HEADS):
            span = slice(half * ROWS + h * RUN, half * ROWS + (h + 1) * RUN)
            parts = [(own_ref[0:HD, span], own_ref[HD : HD + 1, span], own_ref[HD + 8 : HD + 9, span])]
            within = slice(h * RUN, (h + 1) * RUN)
            for ref, at in ((one_ref, span), (two_ref, span), ((low_ref, high_ref)[half], within)):
                tail = ref[HD:ACC, at].astype(jnp.float32)
                parts.append(
                    (
                        ref[0:HD, at].astype(jnp.float32),
                        tail[0:1] + tail[1:2] + tail[2:3],
                        tail[3:4] + tail[4:5] + tail[5:6],
                    )
                )
            top = functools.reduce(jnp.maximum, [p[2] for p in parts])
            factors = [jnp.exp2(p[2] - top) for p in parts]
            numer = sum(p[0] * f for p, f in zip(parts, factors))
            total = sum(p[1] * f for p, f in zip(parts, factors))
            out_ref[half * RUN : (half + 1) * RUN, h * HD : (h + 1) * HD] = (
                (numer / total).T.astype(jnp.bfloat16)
            )


def combine(own, others):
    return pl.pallas_call(
        combine_kernel,
        out_shape=jax.ShapeDtypeStruct((2 * RUN, ROWS), jnp.bfloat16),
        in_specs=[pl.BlockSpec(memory_space=pltpu.VMEM)] * 5,
        out_specs=pl.BlockSpec(memory_space=pltpu.VMEM),
        compiler_params=pltpu.CompilerParams(vmem_limit_bytes=VMEM_BYTES),
        name="combine",
    )(own, *others)


def place_of(x, y, z, core):
    return ((x // 2) * 2 + core) * 32 + (y * 4 + z) * 2 + x % 2


def swap(array, flips):
    pairs = []
    for x in range(4):
        for y in range(4):
            for z in range(4):
                for core in range(2):
                    dx, dy, dz, dc = flips(core)
                    pairs.append((place_of(x, y, z, core), place_of(x ^ dx, y ^ dy, z ^ dz, core ^ dc)))
    return lax.ppermute(array, AXES, pairs)


def ring_x(array, step):
    return swap(array, lambda core: (step, 0, 0, 0))


def ring_first(array, step):
    return swap(array, lambda core: (0, step, 0, 0) if core else (0, 0, step, 0))


def ring_second(array, step):
    return swap(array, lambda core: (0, 0, step, 0) if core else (0, step, 0, 0))


def cores(array):
    return swap(array, lambda core: (0, 0, 0, 1))


def body(queries, keys, values, positions):
    shard = pack_kv(positions, keys, values)
    near = [ring_first(shard, s) for s in (1, 3, 2)]
    packed, acc0 = pack_q(queries, shard)
    near, _ = lax.optimization_barrier((near, packed))
    line = jnp.concatenate([shard] + near, axis=0)
    q2 = ring_x(packed, 2)
    far1, far3 = ring_second(line, 1), ring_second(line, 3)
    line_x = cores(line)
    (acc_own,) = attend([packed], [line, line_x], base=acc0, final=False)
    far1, far3, q2, line_x, line, packed, acc_own = lax.optimization_barrier(
        (far1, far3, q2, line_x, line, packed, acc_own)
    )
    far2 = ring_second(line, 2)
    q1, q3 = ring_x(packed, 1), ring_x(packed, 3)
    first = [line, line_x, far1, far3, cores(far1), cores(far3)]
    (acc2,) = attend([q2], first, final=False)
    far2, acc2 = lax.optimization_barrier((far2, acc2))
    last = [far2, cores(far2)]
    part2, *whole = attend([q2], last, first, acc=[acc2], keep=True)
    q1, q3, part2 = lax.optimization_barrier((q1, q3, part2))
    back2 = ring_x(part2, 2)
    part1, low3 = attend([q1, q3], given=whole, only=(None, 0))
    q3, part1, low3 = lax.optimization_barrier((q3, part1, low3))
    back1, back_low = ring_x(part1, 1), ring_x(low3, 3)
    (high3,) = attend([q3], given=whole, only=(1,))
    high3, back2 = lax.optimization_barrier((high3, back2))
    packed, high3 = lax.optimization_barrier((packed, high3))
    back_high = ring_x(high3, 3)
    packed, back_low = lax.optimization_barrier((packed, back_low))
    (mine,) = attend([packed], given=whole, acc=[acc_own], base=acc0, done=8)
    return combine(mine, (back1, back2, back_low, back_high))


def solution(mesh):
    return jax.shard_map(
        body,
        mesh=mesh,
        in_specs=(P(AXES, None), P(AXES, None), P(AXES, None), P(AXES)),
        out_specs=P(AXES, None),
        check_vma=False,
    )
```

```python
import functools
import math

import jax
import jax.numpy as jnp
from jax import lax
from jax.experimental import pallas as pl
from jax.experimental.pallas import tpu as pltpu
from jax.sharding import PartitionSpec as P

AXES = ("outer", "inner")
RUN = 128
HD = 128
HEADS = 8
ROWS = RUN * HEADS
SHARD = 4 * RUN + 16
QROWS = 2 * RUN + 16
ACC = HD + 16
COEF = HD**-0.5 * math.log2(math.e)
NEG = -1e30
LIMIT = 2.0**100
VMEM_BYTES = 22 * 2**20


def dot(a, b, ca, cb):
    return lax.dot_general(a, b, (((ca,), (cb,)), ((), ())), preferred_element_type=jnp.float32)


def split3(x):
    hi = x.astype(jnp.bfloat16)
    rest = x - hi.astype(jnp.float32)
    mid = rest.astype(jnp.bfloat16)
    low = (rest - mid.astype(jnp.float32)).astype(jnp.bfloat16)
    return hi, mid, low


def stack_rows(rows, width):
    at = lax.broadcasted_iota(jnp.int32, (16, width), 0)
    tile = jnp.zeros((16, width), jnp.float32)
    for i, row in enumerate(rows):
        tile = jnp.where(at == i, row.astype(jnp.float32), tile)
    return tile.astype(jnp.bfloat16)


def pack_kv_kernel(pos_ref, key_ref, value_ref, out_ref):
    out_ref[0 : 2 * RUN, :] = key_ref[...]
    for half in range(2):
        v = value_ref[half * RUN : (half + 1) * RUN, :].astype(jnp.float32)
        out_ref[(2 + half) * RUN : (3 + half) * RUN, :] = v.T.astype(jnp.bfloat16)
    block = (pos_ref[0] // RUN).astype(jnp.float32)
    out_ref[4 * RUN : SHARD, :] = jnp.full((16, HD), block, jnp.float32).astype(jnp.bfloat16)


def pack_kv(positions, keys, values):
    return pl.pallas_call(
        pack_kv_kernel,
        out_shape=jax.ShapeDtypeStruct((SHARD, HD), jnp.bfloat16),
        in_specs=[
            pl.BlockSpec(memory_space=pltpu.SMEM),
            pl.BlockSpec(memory_space=pltpu.VMEM),
            pl.BlockSpec(memory_space=pltpu.VMEM),
        ],
        out_specs=pl.BlockSpec(memory_space=pltpu.VMEM),
        name="pack_kv",
    )(positions, keys, values)


def query_tile(ref, half):
    rows = slice(half * RUN, (half + 1) * RUN)
    return jnp.concatenate([ref[rows, h * HD : (h + 1) * HD] for h in range(HEADS)], axis=0)


def pack_q_kernel(query_ref, shard_ref, out_ref, acc_ref):
    out_ref[0 : 2 * RUN, :] = query_ref[...]
    shifts = []
    key_at = lax.broadcasted_iota(jnp.int32, (RUN, ROWS), 0)
    row_at = lax.broadcasted_iota(jnp.int32, (RUN, ROWS), 1) % RUN
    ones = jnp.ones((16, RUN), jnp.bfloat16)
    for half in range(2):
        scores = dot(shard_ref[half * RUN : (half + 1) * RUN, :], query_tile(query_ref, half), 1, 1)
        scores = jnp.where(key_at <= row_at, scores * COEF, NEG)
        shift = jnp.max(scores, axis=0, keepdims=True)
        weights = jnp.exp2(scores - shift).astype(jnp.bfloat16)
        vt = jnp.concatenate([shard_ref[(2 + half) * RUN : (3 + half) * RUN, :], ones], axis=0)
        acc_ref[:, half * ROWS : (half + 1) * ROWS] = dot(vt, weights, 1, 0)
        shifts.append(shift)
    block = jnp.concatenate([shard_ref[4 * RUN : 4 * RUN + 1, :]] * HEADS, axis=1)
    out_ref[2 * RUN : QROWS, :] = stack_rows(split3(shifts[0]) + split3(shifts[1]) + (block,), ROWS)


def pack_q(queries, shard):
    return pl.pallas_call(
        pack_q_kernel,
        out_shape=(
            jax.ShapeDtypeStruct((QROWS, ROWS), jnp.bfloat16),
            jax.ShapeDtypeStruct((ACC, 2 * ROWS), jnp.float32),
        ),
        in_specs=[pl.BlockSpec(memory_space=pltpu.VMEM)] * 2,
        out_specs=(pl.BlockSpec(memory_space=pltpu.VMEM),) * 2,
        compiler_params=pltpu.CompilerParams(vmem_limit_bytes=VMEM_BYTES),
        name="pack_q",
    )(queries, shard)


def attend_kernel(count, sizes, old, done, only, have, base, final, keep, given, *refs):
    whole_only = only
    q_refs = refs[:count]
    at = count
    piece_refs = () if given else refs[at : at + len(sizes)]
    at += len(piece_refs)
    if given:
        kv_ref, numbers = refs[at : at + 2]
        at += 2
    in_refs = refs[at : at + count] if have else None
    at += count if have else 0
    base_ref = refs[at] if base else None
    at += 1 if base else 0
    carry_in = refs[at] if 1 in only else None
    at += 1 if 1 in only else 0
    out_refs = refs[at : at + count]
    at += count
    carry_out = refs[at] if 0 in only else None
    at += 1 if 0 in only else 0
    if keep:
        kv_ref, numbers = refs[at : at + 2]
        at += 2
    elif not given:
        kv_ref, numbers = refs[at : at + 2]
        at += 2
    q_buf, m_buf, acc_ref, tasks = refs[at : at + 4]
    ints, blocks, sems, sem = (None,) * 4 if given else refs[at + 4 :]
    starts = [sum(sizes[:i]) for i in range(len(sizes) + 1)]
    shards = starts[-1]
    group = 16 if shards - done >= 24 else 8

    def piece_copy(i):
        there = kv_ref.at[pl.ds(starts[i] * SHARD, sizes[i] * SHARD), :]
        return pltpu.make_async_copy(piece_refs[i], there, sems.at[i])

    def read_blocks(first, last):
        for i in range(first, last):
            row = kv_ref[i * SHARD + 4 * RUN : i * SHARD + SHARD, :].astype(jnp.float32)[0:1]
            ints[i : i + 1, :] = row.astype(jnp.int32)
        copy = pltpu.make_async_copy(ints, blocks, sem)
        copy.start()
        copy.wait()
        for i in range(first, last):
            numbers[i] = blocks[i, 0]

    if not given:
        for i in list(range(old, len(sizes))) + (list(range(old)) if keep else []):
            piece_copy(i).start()

    def key_block(task):
        shard = task // 2
        start = pl.multiple_of(shard * SHARD + (task - 2 * shard) * RUN, 16)
        return kv_ref[pl.ds(start, RUN), :]

    def value_block(task):
        shard = task // 2
        start = pl.multiple_of(shard * SHARD + (2 + task - 2 * shard) * RUN, 16)
        return kv_ref[pl.ds(start, RUN), :]

    def list_tasks(here, first, last):
        total = 2 * (last - first)

        def place(i, ends):
            low, high = ends
            block = numbers[i]
            tasks[high] = 2 * i
            high = high - 1
            later = block > here
            tasks[jnp.where(later, high, total)] = 2 * i + 1
            high = high - later.astype(jnp.int32)
            earlier = block < here
            tasks[jnp.where(earlier, low, total)] = 2 * i
            low = low + earlier.astype(jnp.int32)
            return low, high

        for i in range(total):
            tasks[i] = 2 * first
        low_end, high_end = lax.fori_loop(first, last, place, (jnp.int32(0), jnp.int32(total - 1)))
        return low_end, high_end + 1

    ones = jnp.ones((16, group * RUN), jnp.bfloat16)

    for j in range(count):
        only = whole_only[j]
        halves = (0, 1) if only is None else (only,)
        touched = (1,) if only == 1 else (0, 1)
        q_ref = q_refs[j]
        tail = q_ref[2 * RUN : QROWS, :].astype(jnp.float32)
        for half in touched:
            span = slice(half * ROWS, (half + 1) * ROWS)
            q_buf[half] = query_tile(q_ref, half)
            m_buf[half] = jnp.broadcast_to(
                tail[3 * half : 3 * half + 1]
                + tail[3 * half + 1 : 3 * half + 2]
                + tail[3 * half + 2 : 3 * half + 3],
                (8, ROWS),
            )
            if have:
                acc_ref[half] = in_refs[j][:, span]
            elif base:
                acc_ref[half] = base_ref[:, span]
            elif only == 1:
                acc_ref[half] = carry_in[...]
            else:
                acc_ref[half] = jnp.zeros((ACC, ROWS), jnp.float32)
        here = jnp.max(tail[6:7, 0:HD]).astype(jnp.int32)
        if j == 0 and not given:
            for i in range(old, len(sizes)):
                piece_copy(i).wait()
            read_blocks(starts[old], shards)
        low_end, high_start = list_tasks(here, done, shards)

        def pure(first, half, group):
            query = q_buf[half]
            shift = m_buf[half][0:1]
            parts = []
            for b in range(0, group, 2):
                keys = jnp.concatenate([key_block(tasks[first + b]), key_block(tasks[first + b + 1])], axis=0)
                parts.append(jnp.exp2(dot(keys, query, 1, 1) * COEF - shift).astype(jnp.bfloat16))
            weights = jnp.concatenate(parts, axis=0)
            vt = jnp.concatenate([value_block(tasks[first + b]) for b in range(group)], axis=1)
            vt = jnp.concatenate([vt, ones[:, : group * RUN]], axis=0)
            acc_ref[half] += dot(vt, weights, 1, 0)

        def mixed(first, group):
            parts = []
            for b in range(group):
                half = (first + b >= high_start).astype(jnp.int32)
                scores = dot(key_block(tasks[first + b]), q_buf[half], 1, 1)
                parts.append(jnp.exp2(scores * COEF - m_buf[half][0:1]).astype(jnp.bfloat16))
            weights = jnp.concatenate(parts, axis=0)
            vt = jnp.concatenate([value_block(tasks[first + b]) for b in range(group)], axis=1)
            vt = jnp.concatenate([vt, ones[:, : group * RUN]], axis=0)
            index = first + lax.broadcasted_iota(jnp.int32, (1, group * RUN), 1) // RUN
            zero = jnp.zeros((), jnp.bfloat16)
            acc_ref[0] += dot(jnp.where(index < low_end, vt, zero), weights, 1, 0)
            acc_ref[1] += dot(jnp.where(index >= high_start, vt, zero), weights, 1, 0)

        steps = 2 * (shards - done) // group

        @pl.loop(steps // 2 if only == 1 else 0, steps // 2 if only == 0 else steps)
        def _(g):
            first = g * group
            is_low = first + group <= low_end
            is_high = first >= high_start

            if only == 1:
                pure(first, 1, group)
                return

            @pl.when(jnp.logical_or(is_low, is_high))
            def _():
                pure(first, is_high.astype(jnp.int32), group)

            @pl.when(jnp.logical_not(jnp.logical_or(is_low, is_high)))
            def _():
                @pl.loop(0, group // 8)
                def _(part):
                    begin = first + part * 8
                    low_8 = begin + 8 <= low_end
                    high_8 = begin >= high_start
                    pure_8 = jnp.logical_or(low_8, high_8)

                    @pl.when(pure_8)
                    def _():
                        pure(begin, high_8.astype(jnp.int32), 8)

                    @pl.when(jnp.logical_not(pure_8))
                    def _():
                        mixed(begin, 8)

        if only == 0:
            carry_out[...] = acc_ref[1]

        if keep and old:
            for i in range(old):
                piece_copy(i).wait()
            read_blocks(0, starts[old])

        if not final:
            for half in range(2):
                out_refs[j][:, half * ROWS : (half + 1) * ROWS] = acc_ref[half]
            continue

        sums = functools.reduce(jnp.maximum, [acc_ref[half][HD : HD + 8] for half in halves])
        fine = jnp.min(jnp.where(sums < LIMIT, 1.0, 0.0)) > 0.5

        @pl.when(jnp.logical_not(fine))
        def _():
            if old and not keep:
                for i in range(old):
                    piece_copy(i).start()
                for i in range(old):
                    piece_copy(i).wait()
                read_blocks(0, starts[old])
            low_all, high_all = list_tasks(here, 0, shards)
            for half in halves:
                if base:
                    acc_ref[half] = base_ref[:, half * ROWS : (half + 1) * ROWS]
                else:
                    acc_ref[half] = jnp.zeros((ACC, ROWS), jnp.float32)

            @pl.loop(0, 2 * shards)
            def _(t):
                in_low = jnp.logical_and(t < low_all, only != 1)
                in_high = jnp.logical_and(t >= high_all, only != 0)

                @pl.when(jnp.logical_or(in_low, in_high))
                def _():
                    half = (t >= high_all).astype(jnp.int32) if only is None else only
                    scores = dot(key_block(tasks[t]), q_buf[half], 1, 1) * COEF
                    before = m_buf[half][0:1]
                    new = jnp.maximum(before, jnp.max(scores, axis=0, keepdims=True))
                    weights = jnp.exp2(scores - new).astype(jnp.bfloat16)
                    vt = jnp.concatenate([value_block(tasks[t]), ones[:, :RUN]], axis=0)
                    acc_ref[half] = acc_ref[half] * jnp.exp2(before - new) + dot(vt, weights, 1, 0)
                    m_buf[half] = jnp.broadcast_to(new, (8, ROWS))

        for half in halves:
            span = slice(half * ROWS, (half + 1) * ROWS) if only is None else slice(0, ROWS)
            if base:
                out_refs[j][0 : HD + 8, span] = acc_ref[half][0 : HD + 8]
                out_refs[j][HD + 8 : ACC, span] = m_buf[half]
            else:
                acc = acc_ref[half]
                out_refs[j][0:HD, span] = acc[0:HD].astype(jnp.bfloat16)
                out_refs[j][HD:ACC, span] = stack_rows(
                    split3(acc[HD : HD + 1]) + split3(m_buf[half][0:1]), ROWS
                )


def attend(q_list, new=(), old=(), acc=None, base=None, final=True, keep=False, given=None, done=0, only=None, carry=None):
    only = only or (None,) * len(q_list)
    count = len(q_list)
    pieces = (tuple(old) if final else ()) + tuple(new)
    skip = len(old) if final else 0
    sizes = tuple(p.shape[0] // SHARD for p in pieces) if given is None else (given[0].shape[0] // SHARD,)
    shards = sum(sizes)
    done = done if given is not None else sum(sizes[:skip])
    int_rows = -(-shards // 8) * 8
    vmem, smem = pl.BlockSpec(memory_space=pltpu.VMEM), pl.BlockSpec(memory_space=pltpu.SMEM)
    args = list(q_list) + list(pieces)
    in_specs = [vmem] * count + [pl.BlockSpec(memory_space=pl.ANY)] * len(pieces)
    if given is not None:
        args += given
        in_specs += [vmem, smem]
    if acc is not None:
        args += acc
        in_specs += [vmem] * count
    if base is not None:
        args.append(base)
        in_specs.append(vmem)
    if carry is not None:
        args.append(carry)
        in_specs.append(vmem)
    kind = jnp.bfloat16 if final and base is None else jnp.float32
    outs = [jax.ShapeDtypeStruct((ACC, (2 if run is None else 1) * ROWS), kind) for run in only]
    out_specs = [vmem] * count
    if 0 in only:
        outs.append(jax.ShapeDtypeStruct((ACC, ROWS), jnp.float32))
        out_specs.append(vmem)
    scratch = []
    if keep:
        outs += [
            jax.ShapeDtypeStruct((shards * SHARD, HD), jnp.bfloat16),
            jax.ShapeDtypeStruct((int_rows,), jnp.int32),
        ]
        out_specs += [vmem, smem]
    elif given is None:
        scratch += [pltpu.VMEM((shards * SHARD, HD), jnp.bfloat16), pltpu.SMEM((int_rows,), jnp.int32)]
    scratch += [
        pltpu.VMEM((2, ROWS, HD), jnp.bfloat16),
        pltpu.VMEM((2, 8, ROWS), jnp.float32),
        pltpu.VMEM((2, ACC, ROWS), jnp.float32),
        pltpu.SMEM((2 * shards + 8,), jnp.int32),
    ]
    if given is None:
        scratch += [
            pltpu.VMEM((int_rows, HD), jnp.int32),
            pltpu.SMEM((int_rows, HD), jnp.int32),
            pltpu.SemaphoreType.DMA((len(pieces),)),
            pltpu.SemaphoreType.DMA,
        ]
    pairs = count * 2 * (shards - done) * RUN * ROWS
    flags = (count, sizes, skip, done, only, acc is not None, base is not None, final, keep, given is not None)
    return pl.pallas_call(
        functools.partial(attend_kernel, *flags),
        out_shape=outs,
        in_specs=in_specs,
        out_specs=out_specs,
        scratch_shapes=scratch,
        compiler_params=pltpu.CompilerParams(vmem_limit_bytes=VMEM_BYTES),
        cost_estimate=pl.CostEstimate(flops=pairs, bytes_accessed=1 << 20, transcendentals=0),
        name="attend",
    )(*args)


def combine_kernel(own_ref, one_ref, two_ref, low_ref, high_ref, out_ref):
    for half in range(2):
        for h in range(HEADS):
            span = slice(half * ROWS + h * RUN, half * ROWS + (h + 1) * RUN)
            parts = [(own_ref[0:HD, span], own_ref[HD : HD + 1, span], own_ref[HD + 8 : HD + 9, span])]
            within = slice(h * RUN, (h + 1) * RUN)
            for ref, at in ((one_ref, span), (two_ref, span), ((low_ref, high_ref)[half], within)):
                tail = ref[HD:ACC, at].astype(jnp.float32)
                parts.append(
                    (
                        ref[0:HD, at].astype(jnp.float32),
                        tail[0:1] + tail[1:2] + tail[2:3],
                        tail[3:4] + tail[4:5] + tail[5:6],
                    )
                )
            top = functools.reduce(jnp.maximum, [p[2] for p in parts])
            factors = [jnp.exp2(p[2] - top) for p in parts]
            numer = sum(p[0] * f for p, f in zip(parts, factors))
            total = sum(p[1] * f for p, f in zip(parts, factors))
            out_ref[half * RUN : (half + 1) * RUN, h * HD : (h + 1) * HD] = (
                (numer / total).T.astype(jnp.bfloat16)
            )


def combine(own, others):
    return pl.pallas_call(
        combine_kernel,
        out_shape=jax.ShapeDtypeStruct((2 * RUN, ROWS), jnp.bfloat16),
        in_specs=[pl.BlockSpec(memory_space=pltpu.VMEM)] * 5,
        out_specs=pl.BlockSpec(memory_space=pltpu.VMEM),
        compiler_params=pltpu.CompilerParams(vmem_limit_bytes=VMEM_BYTES),
        name="combine",
    )(own, *others)


def place_of(x, y, z, core):
    return ((x // 2) * 2 + core) * 32 + (y * 4 + z) * 2 + x % 2


def swap(array, flips):
    pairs = []
    for x in range(4):
        for y in range(4):
            for z in range(4):
                for core in range(2):
                    dx, dy, dz, dc = flips(core)
                    pairs.append((place_of(x, y, z, core), place_of(x ^ dx, y ^ dy, z ^ dz, core ^ dc)))
    return lax.ppermute(array, AXES, pairs)


def ring_x(array, step):
    return swap(array, lambda core: (step, 0, 0, 0))


def ring_first(array, step):
    return swap(array, lambda core: (0, step, 0, 0) if core else (0, 0, step, 0))


def ring_second(array, step):
    return swap(array, lambda core: (0, 0, step, 0) if core else (0, step, 0, 0))


def cores(array):
    return swap(array, lambda core: (0, 0, 0, 1))


def body(queries, keys, values, positions):
    shard = pack_kv(positions, keys, values)
    near = [ring_first(shard, s) for s in (2, 3, 1)]
    packed, acc0 = pack_q(queries, shard)
    near, _ = lax.optimization_barrier((near, packed))
    line = jnp.concatenate([shard] + near, axis=0)
    q2 = ring_x(packed, 2)
    far1, far3 = ring_second(line, 1), ring_second(line, 3)
    line_x = cores(line)
    (acc_own,) = attend([packed], [line, line_x], base=acc0, final=False)
    far1, far3, q2, line_x, line, packed, acc_own = lax.optimization_barrier(
        (far1, far3, q2, line_x, line, packed, acc_own)
    )
    far2 = ring_second(line, 2)
    q1, q3 = ring_x(packed, 1), ring_x(packed, 3)
    first = [line, line_x, far1, far3, cores(far1), cores(far3)]
    (acc2,) = attend([q2], first, final=False)
    far2, acc2 = lax.optimization_barrier((far2, acc2))
    last = [far2, cores(far2)]
    part2, *whole = attend([q2], last, first, acc=[acc2], keep=True)
    q1, q3, part2 = lax.optimization_barrier((q1, q3, part2))
    back2 = ring_x(part2, 2)
    part1, low3, carry = attend([q1, q3], given=whole, only=(None, 0))
    q3, part1, low3, carry = lax.optimization_barrier((q3, part1, low3, carry))
    back1, back_low = ring_x(part1, 1), ring_x(low3, 3)
    (high3,) = attend([q3], given=whole, only=(1,), carry=carry)
    high3, back2 = lax.optimization_barrier((high3, back2))
    packed, high3 = lax.optimization_barrier((packed, high3))
    back_high = ring_x(high3, 3)
    packed, back_low = lax.optimization_barrier((packed, back_low))
    (mine,) = attend([packed], given=whole, acc=[acc_own], base=acc0, done=8)
    return combine(mine, (back1, back2, back_low, back_high))


def solution(mesh):
    return jax.shard_map(
        body,
        mesh=mesh,
        in_specs=(P(AXES, None), P(AXES, None), P(AXES, None), P(AXES)),
        out_specs=P(AXES, None),
        check_vma=False,
    )
```

```python
import functools
import math

import jax
import jax.numpy as jnp
from jax import lax
from jax.experimental import pallas as pl
from jax.experimental.pallas import tpu as pltpu
from jax.sharding import PartitionSpec as P

AXES = ("outer", "inner")
RUN = 128
HD = 128
HEADS = 8
ROWS = RUN * HEADS
SHARD = 4 * RUN + 16
QROWS = 2 * RUN + 16
ACC = HD + 16
COEF = HD**-0.5 * math.log2(math.e)
NEG = -1e30
LIMIT = 2.0**100
VMEM_BYTES = 22 * 2**20


def dot(a, b, ca, cb):
    return lax.dot_general(a, b, (((ca,), (cb,)), ((), ())), preferred_element_type=jnp.float32)


def split3(x):
    hi = x.astype(jnp.bfloat16)
    rest = x - hi.astype(jnp.float32)
    mid = rest.astype(jnp.bfloat16)
    low = (rest - mid.astype(jnp.float32)).astype(jnp.bfloat16)
    return hi, mid, low


def stack_rows(rows, width):
    at = lax.broadcasted_iota(jnp.int32, (16, width), 0)
    tile = jnp.zeros((16, width), jnp.float32)
    for i, row in enumerate(rows):
        tile = jnp.where(at == i, row.astype(jnp.float32), tile)
    return tile.astype(jnp.bfloat16)


def pack_kv_kernel(pos_ref, key_ref, value_ref, out_ref):
    out_ref[0 : 2 * RUN, :] = key_ref[...]
    for half in range(2):
        v = value_ref[half * RUN : (half + 1) * RUN, :].astype(jnp.float32)
        out_ref[(2 + half) * RUN : (3 + half) * RUN, :] = v.T.astype(jnp.bfloat16)
    block = (pos_ref[0] // RUN).astype(jnp.float32)
    out_ref[4 * RUN : SHARD, :] = jnp.full((16, HD), block, jnp.float32).astype(jnp.bfloat16)


def pack_kv(positions, keys, values):
    return pl.pallas_call(
        pack_kv_kernel,
        out_shape=jax.ShapeDtypeStruct((SHARD, HD), jnp.bfloat16),
        in_specs=[
            pl.BlockSpec(memory_space=pltpu.SMEM),
            pl.BlockSpec(memory_space=pltpu.VMEM),
            pl.BlockSpec(memory_space=pltpu.VMEM),
        ],
        out_specs=pl.BlockSpec(memory_space=pltpu.VMEM),
        name="pack_kv",
    )(positions, keys, values)


def query_tile(ref, half):
    rows = slice(half * RUN, (half + 1) * RUN)
    return jnp.concatenate([ref[rows, h * HD : (h + 1) * HD] for h in range(HEADS)], axis=0)


def pack_q_kernel(query_ref, shard_ref, out_ref, acc_ref):
    out_ref[0 : 2 * RUN, :] = query_ref[...]
    shifts = []
    key_at = lax.broadcasted_iota(jnp.int32, (RUN, ROWS), 0)
    row_at = lax.broadcasted_iota(jnp.int32, (RUN, ROWS), 1) % RUN
    ones = jnp.ones((16, RUN), jnp.bfloat16)
    for half in range(2):
        scores = dot(shard_ref[half * RUN : (half + 1) * RUN, :], query_tile(query_ref, half), 1, 1)
        scores = jnp.where(key_at <= row_at, scores * COEF, NEG)
        shift = jnp.max(scores, axis=0, keepdims=True)
        weights = jnp.exp2(scores - shift).astype(jnp.bfloat16)
        vt = jnp.concatenate([shard_ref[(2 + half) * RUN : (3 + half) * RUN, :], ones], axis=0)
        acc_ref[:, half * ROWS : (half + 1) * ROWS] = dot(vt, weights, 1, 0)
        shifts.append(shift)
    block = jnp.concatenate([shard_ref[4 * RUN : 4 * RUN + 1, :]] * HEADS, axis=1)
    out_ref[2 * RUN : QROWS, :] = stack_rows(split3(shifts[0]) + split3(shifts[1]) + (block,), ROWS)


def pack_q(queries, shard):
    return pl.pallas_call(
        pack_q_kernel,
        out_shape=(
            jax.ShapeDtypeStruct((QROWS, ROWS), jnp.bfloat16),
            jax.ShapeDtypeStruct((ACC, 2 * ROWS), jnp.float32),
        ),
        in_specs=[pl.BlockSpec(memory_space=pltpu.VMEM)] * 2,
        out_specs=(pl.BlockSpec(memory_space=pltpu.VMEM),) * 2,
        compiler_params=pltpu.CompilerParams(vmem_limit_bytes=VMEM_BYTES),
        name="pack_q",
    )(queries, shard)


def attend_kernel(count, sizes, old, done, only, have, base, final, keep, given, *refs):
    whole_only = only
    q_refs = refs[:count]
    at = count
    piece_refs = () if given else refs[at : at + len(sizes)]
    at += len(piece_refs)
    if given:
        kv_ref, numbers = refs[at : at + 2]
        at += 2
    in_refs = refs[at : at + count] if have else None
    at += count if have else 0
    base_ref = refs[at] if base else None
    at += 1 if base else 0
    carry_in = refs[at] if 1 in only else None
    at += 1 if 1 in only else 0
    out_refs = refs[at : at + count]
    at += count
    carry_out = refs[at] if 0 in only else None
    at += 1 if 0 in only else 0
    if keep:
        kv_ref, numbers = refs[at : at + 2]
        at += 2
    elif not given:
        kv_ref, numbers = refs[at : at + 2]
        at += 2
    q_buf, m_buf, acc_ref, tasks = refs[at : at + 4]
    ints, blocks, sems, sem = (None,) * 4 if given else refs[at + 4 :]
    starts = [sum(sizes[:i]) for i in range(len(sizes) + 1)]
    shards = starts[-1]
    group = 16 if shards - done >= 24 else 8

    def piece_copy(i):
        there = kv_ref.at[pl.ds(starts[i] * SHARD, sizes[i] * SHARD), :]
        return pltpu.make_async_copy(piece_refs[i], there, sems.at[i])

    def read_blocks(first, last):
        for i in range(first, last):
            row = kv_ref[i * SHARD + 4 * RUN : i * SHARD + SHARD, :].astype(jnp.float32)[0:1]
            ints[i : i + 1, :] = row.astype(jnp.int32)
        copy = pltpu.make_async_copy(ints, blocks, sem)
        copy.start()
        copy.wait()
        for i in range(first, last):
            numbers[i] = blocks[i, 0]

    if not given:
        for i in list(range(old, len(sizes))) + (list(range(old)) if keep else []):
            piece_copy(i).start()

    def key_block(task):
        shard = task // 2
        start = pl.multiple_of(shard * SHARD + (task - 2 * shard) * RUN, 16)
        return kv_ref[pl.ds(start, RUN), :]

    def value_block(task):
        shard = task // 2
        start = pl.multiple_of(shard * SHARD + (2 + task - 2 * shard) * RUN, 16)
        return kv_ref[pl.ds(start, RUN), :]

    def list_tasks(here, first, last):
        total = 2 * (last - first)

        def place(i, ends):
            low, high = ends
            block = numbers[i]
            tasks[high] = 2 * i
            high = high - 1
            later = block > here
            tasks[jnp.where(later, high, total)] = 2 * i + 1
            high = high - later.astype(jnp.int32)
            earlier = block < here
            tasks[jnp.where(earlier, low, total)] = 2 * i
            low = low + earlier.astype(jnp.int32)
            return low, high

        for i in range(total):
            tasks[i] = 2 * first
        low_end, high_end = lax.fori_loop(first, last, place, (jnp.int32(0), jnp.int32(total - 1)), unroll=4)
        return low_end, high_end + 1

    ones = jnp.ones((16, group * RUN), jnp.bfloat16)

    for j in range(count):
        only = whole_only[j]
        halves = (0, 1) if only is None else (only,)
        touched = (1,) if only == 1 else (0, 1)
        q_ref = q_refs[j]
        tail = q_ref[2 * RUN : QROWS, :].astype(jnp.float32)
        for half in touched:
            span = slice(half * ROWS, (half + 1) * ROWS)
            q_buf[half] = query_tile(q_ref, half)
            m_buf[half] = jnp.broadcast_to(
                tail[3 * half : 3 * half + 1]
                + tail[3 * half + 1 : 3 * half + 2]
                + tail[3 * half + 2 : 3 * half + 3],
                (8, ROWS),
            )
            if have:
                acc_ref[half] = in_refs[j][:, span]
            elif base:
                acc_ref[half] = base_ref[:, span]
            elif only == 1:
                acc_ref[half] = carry_in[...]
            else:
                acc_ref[half] = jnp.zeros((ACC, ROWS), jnp.float32)
        here = jnp.max(tail[6:7, 0:HD]).astype(jnp.int32)
        if j == 0 and not given:
            for i in range(old, len(sizes)):
                piece_copy(i).wait()
            read_blocks(starts[old], shards)
        low_end, high_start = list_tasks(here, done, shards)

        def pure(first, half, group):
            query = q_buf[half]
            shift = m_buf[half][0:1]
            parts = []
            for b in range(0, group, 2):
                keys = jnp.concatenate([key_block(tasks[first + b]), key_block(tasks[first + b + 1])], axis=0)
                parts.append(jnp.exp2(dot(keys, query, 1, 1) * COEF - shift).astype(jnp.bfloat16))
            weights = jnp.concatenate(parts, axis=0)
            vt = jnp.concatenate([value_block(tasks[first + b]) for b in range(group)], axis=1)
            vt = jnp.concatenate([vt, ones[:, : group * RUN]], axis=0)
            acc_ref[half] += dot(vt, weights, 1, 0)

        def mixed(first, group):
            parts = []
            for b in range(group):
                half = (first + b >= high_start).astype(jnp.int32)
                scores = dot(key_block(tasks[first + b]), q_buf[half], 1, 1)
                parts.append(jnp.exp2(scores * COEF - m_buf[half][0:1]).astype(jnp.bfloat16))
            weights = jnp.concatenate(parts, axis=0)
            vt = jnp.concatenate([value_block(tasks[first + b]) for b in range(group)], axis=1)
            vt = jnp.concatenate([vt, ones[:, : group * RUN]], axis=0)
            index = first + lax.broadcasted_iota(jnp.int32, (1, group * RUN), 1) // RUN
            zero = jnp.zeros((), jnp.bfloat16)
            acc_ref[0] += dot(jnp.where(index < low_end, vt, zero), weights, 1, 0)
            acc_ref[1] += dot(jnp.where(index >= high_start, vt, zero), weights, 1, 0)

        steps = 2 * (shards - done) // group

        @pl.loop(steps // 2 if only == 1 else 0, steps // 2 if only == 0 else steps)
        def _(g):
            first = g * group
            is_low = first + group <= low_end
            is_high = first >= high_start

            if only == 1:
                pure(first, 1, group)
                return

            @pl.when(jnp.logical_or(is_low, is_high))
            def _():
                pure(first, is_high.astype(jnp.int32), group)

            @pl.when(jnp.logical_not(jnp.logical_or(is_low, is_high)))
            def _():
                @pl.loop(0, group // 8)
                def _(part):
                    begin = first + part * 8
                    low_8 = begin + 8 <= low_end
                    high_8 = begin >= high_start
                    pure_8 = jnp.logical_or(low_8, high_8)

                    @pl.when(pure_8)
                    def _():
                        pure(begin, high_8.astype(jnp.int32), 8)

                    @pl.when(jnp.logical_not(pure_8))
                    def _():
                        mixed(begin, 8)

        if only == 0:
            carry_out[...] = acc_ref[1]

        if keep and old:
            for i in range(old):
                piece_copy(i).wait()
            read_blocks(0, starts[old])

        if not final:
            for half in range(2):
                out_refs[j][:, half * ROWS : (half + 1) * ROWS] = acc_ref[half]
            continue

        sums = functools.reduce(jnp.maximum, [acc_ref[half][HD : HD + 8] for half in halves])
        fine = jnp.min(jnp.where(sums < LIMIT, 1.0, 0.0)) > 0.5

        @pl.when(jnp.logical_not(fine))
        def _():
            if old and not keep:
                for i in range(old):
                    piece_copy(i).start()
                for i in range(old):
                    piece_copy(i).wait()
                read_blocks(0, starts[old])
            low_all, high_all = list_tasks(here, 0, shards)
            for half in halves:
                if base:
                    acc_ref[half] = base_ref[:, half * ROWS : (half + 1) * ROWS]
                else:
                    acc_ref[half] = jnp.zeros((ACC, ROWS), jnp.float32)

            @pl.loop(0, 2 * shards)
            def _(t):
                in_low = jnp.logical_and(t < low_all, only != 1)
                in_high = jnp.logical_and(t >= high_all, only != 0)

                @pl.when(jnp.logical_or(in_low, in_high))
                def _():
                    half = (t >= high_all).astype(jnp.int32) if only is None else only
                    scores = dot(key_block(tasks[t]), q_buf[half], 1, 1) * COEF
                    before = m_buf[half][0:1]
                    new = jnp.maximum(before, jnp.max(scores, axis=0, keepdims=True))
                    weights = jnp.exp2(scores - new).astype(jnp.bfloat16)
                    vt = jnp.concatenate([value_block(tasks[t]), ones[:, :RUN]], axis=0)
                    acc_ref[half] = acc_ref[half] * jnp.exp2(before - new) + dot(vt, weights, 1, 0)
                    m_buf[half] = jnp.broadcast_to(new, (8, ROWS))

        for half in halves:
            span = slice(half * ROWS, (half + 1) * ROWS) if only is None else slice(0, ROWS)
            if base:
                out_refs[j][0 : HD + 8, span] = acc_ref[half][0 : HD + 8]
                out_refs[j][HD + 8 : ACC, span] = m_buf[half]
            else:
                acc = acc_ref[half]
                out_refs[j][0:HD, span] = acc[0:HD].astype(jnp.bfloat16)
                out_refs[j][HD:ACC, span] = stack_rows(
                    split3(acc[HD : HD + 1]) + split3(m_buf[half][0:1]), ROWS
                )


def attend(q_list, new=(), old=(), acc=None, base=None, final=True, keep=False, given=None, done=0, only=None, carry=None):
    only = only or (None,) * len(q_list)
    count = len(q_list)
    pieces = (tuple(old) if final else ()) + tuple(new)
    skip = len(old) if final else 0
    sizes = tuple(p.shape[0] // SHARD for p in pieces) if given is None else (given[0].shape[0] // SHARD,)
    shards = sum(sizes)
    done = done if given is not None else sum(sizes[:skip])
    int_rows = -(-shards // 8) * 8
    vmem, smem = pl.BlockSpec(memory_space=pltpu.VMEM), pl.BlockSpec(memory_space=pltpu.SMEM)
    args = list(q_list) + list(pieces)
    in_specs = [vmem] * count + [pl.BlockSpec(memory_space=pl.ANY)] * len(pieces)
    if given is not None:
        args += given
        in_specs += [vmem, smem]
    if acc is not None:
        args += acc
        in_specs += [vmem] * count
    if base is not None:
        args.append(base)
        in_specs.append(vmem)
    if carry is not None:
        args.append(carry)
        in_specs.append(vmem)
    kind = jnp.bfloat16 if final and base is None else jnp.float32
    outs = [jax.ShapeDtypeStruct((ACC, (2 if run is None else 1) * ROWS), kind) for run in only]
    out_specs = [vmem] * count
    if 0 in only:
        outs.append(jax.ShapeDtypeStruct((ACC, ROWS), jnp.float32))
        out_specs.append(vmem)
    scratch = []
    if keep:
        outs += [
            jax.ShapeDtypeStruct((shards * SHARD, HD), jnp.bfloat16),
            jax.ShapeDtypeStruct((int_rows,), jnp.int32),
        ]
        out_specs += [vmem, smem]
    elif given is None:
        scratch += [pltpu.VMEM((shards * SHARD, HD), jnp.bfloat16), pltpu.SMEM((int_rows,), jnp.int32)]
    scratch += [
        pltpu.VMEM((2, ROWS, HD), jnp.bfloat16),
        pltpu.VMEM((2, 8, ROWS), jnp.float32),
        pltpu.VMEM((2, ACC, ROWS), jnp.float32),
        pltpu.SMEM((2 * shards + 8,), jnp.int32),
    ]
    if given is None:
        scratch += [
            pltpu.VMEM((int_rows, HD), jnp.int32),
            pltpu.SMEM((int_rows, HD), jnp.int32),
            pltpu.SemaphoreType.DMA((len(pieces),)),
            pltpu.SemaphoreType.DMA,
        ]
    pairs = count * 2 * (shards - done) * RUN * ROWS
    flags = (count, sizes, skip, done, only, acc is not None, base is not None, final, keep, given is not None)
    return pl.pallas_call(
        functools.partial(attend_kernel, *flags),
        out_shape=outs,
        in_specs=in_specs,
        out_specs=out_specs,
        scratch_shapes=scratch,
        compiler_params=pltpu.CompilerParams(vmem_limit_bytes=VMEM_BYTES),
        cost_estimate=pl.CostEstimate(flops=pairs, bytes_accessed=1 << 20, transcendentals=0),
        name="attend",
    )(*args)


def combine_kernel(own_ref, one_ref, two_ref, low_ref, high_ref, out_ref):
    for half in range(2):
        for h in range(HEADS):
            span = slice(half * ROWS + h * RUN, half * ROWS + (h + 1) * RUN)
            parts = [(own_ref[0:HD, span], own_ref[HD : HD + 1, span], own_ref[HD + 8 : HD + 9, span])]
            within = slice(h * RUN, (h + 1) * RUN)
            for ref, at in ((one_ref, span), (two_ref, span), ((low_ref, high_ref)[half], within)):
                tail = ref[HD:ACC, at].astype(jnp.float32)
                parts.append(
                    (
                        ref[0:HD, at].astype(jnp.float32),
                        tail[0:1] + tail[1:2] + tail[2:3],
                        tail[3:4] + tail[4:5] + tail[5:6],
                    )
                )
            top = functools.reduce(jnp.maximum, [p[2] for p in parts])
            factors = [jnp.exp2(p[2] - top) for p in parts]
            numer = sum(p[0] * f for p, f in zip(parts, factors))
            total = sum(p[1] * f for p, f in zip(parts, factors))
            out_ref[half * RUN : (half + 1) * RUN, h * HD : (h + 1) * HD] = (
                (numer / total).T.astype(jnp.bfloat16)
            )


def combine(own, others):
    return pl.pallas_call(
        combine_kernel,
        out_shape=jax.ShapeDtypeStruct((2 * RUN, ROWS), jnp.bfloat16),
        in_specs=[pl.BlockSpec(memory_space=pltpu.VMEM)] * 5,
        out_specs=pl.BlockSpec(memory_space=pltpu.VMEM),
        compiler_params=pltpu.CompilerParams(vmem_limit_bytes=VMEM_BYTES),
        name="combine",
    )(own, *others)


def place_of(x, y, z, core):
    return ((x // 2) * 2 + core) * 32 + (y * 4 + z) * 2 + x % 2


def swap(array, flips):
    pairs = []
    for x in range(4):
        for y in range(4):
            for z in range(4):
                for core in range(2):
                    dx, dy, dz, dc = flips(core)
                    pairs.append((place_of(x, y, z, core), place_of(x ^ dx, y ^ dy, z ^ dz, core ^ dc)))
    return lax.ppermute(array, AXES, pairs)


def ring_x(array, step):
    return swap(array, lambda core: (step, 0, 0, 0))


def ring_first(array, step):
    return swap(array, lambda core: (0, step, 0, 0) if core else (0, 0, step, 0))


def ring_second(array, step):
    return swap(array, lambda core: (0, 0, step, 0) if core else (0, step, 0, 0))


def cores(array):
    return swap(array, lambda core: (0, 0, 0, 1))


def body(queries, keys, values, positions):
    shard = pack_kv(positions, keys, values)
    near = [ring_first(shard, s) for s in (2, 3, 1)]
    packed, acc0 = pack_q(queries, shard)
    near, _ = lax.optimization_barrier((near, packed))
    line = jnp.concatenate([shard] + near, axis=0)
    q2 = ring_x(packed, 2)
    far3, far1 = ring_second(line, 3), ring_second(line, 1)
    line_x = cores(line)
    (acc_own,) = attend([packed], [line, line_x], base=acc0, final=False)
    far3, far1, q2, line_x, line, packed, acc_own = lax.optimization_barrier(
        (far3, far1, q2, line_x, line, packed, acc_own)
    )
    far2 = ring_second(line, 2)
    q3, q1 = ring_x(packed, 3), ring_x(packed, 1)
    first = [line, line_x, far1, far3, cores(far1), cores(far3)]
    (acc2,) = attend([q2], first, final=False)
    far2, acc2 = lax.optimization_barrier((far2, acc2))
    last = [far2, cores(far2)]
    part2, *whole = attend([q2], last, first, acc=[acc2], keep=True)
    q3, q1, part2 = lax.optimization_barrier((q3, q1, part2))
    back2 = ring_x(part2, 2)
    part1, low3, carry = attend([q1, q3], given=whole, only=(None, 0))
    q3, part1, low3, carry = lax.optimization_barrier((q3, part1, low3, carry))
    back_low, back1 = ring_x(low3, 3), ring_x(part1, 1)
    (high3,) = attend([q3], given=whole, only=(1,), carry=carry)
    high3, back2 = lax.optimization_barrier((high3, back2))
    packed, high3 = lax.optimization_barrier((packed, high3))
    back_high = ring_x(high3, 3)
    packed, back_low = lax.optimization_barrier((packed, back_low))
    (mine,) = attend([packed], given=whole, acc=[acc_own], base=acc0, done=8)
    return combine(mine, (back1, back2, back_low, back_high))


def solution(mesh):
    return jax.shard_map(
        body,
        mesh=mesh,
        in_specs=(P(AXES, None), P(AXES, None), P(AXES, None), P(AXES)),
        out_specs=P(AXES, None),
        check_vma=False,
    )
```
